256 devices in a mesh: dp: 32 (over z, y), tensor: 8 (over x, core).
Axes of the slice: x: 4, y: 4, z: 8, core: 2. Of those that a mesh axis runs over, the one named last changes fastest.
Arguments:
- hidden: bfloat16 [24576, 14336], P('dp', 'tensor'), may hold values from -6 to 6
- layer_output_gradient: bfloat16 [24576, 4096], P('dp', 'tensor'), may hold values from -6 to 6
- frozen_down_weight: bfloat16 [14336, 4096], P('tensor', 'dp'), may hold values from -0.046875 to 0.046875
- adapter_down_weight: bfloat16 [14336, 128], P('tensor'), may hold values from -0.046875 to 0.046875
- adapter_up_weight: bfloat16 [128, 4096], replicated, may hold values from -0.09375 to 0.09375
- chosen_expert_index: int32 [24576, 2], P('dp'), may hold values from 0 to 7, all different within a row
- gates: float32 [24576, 2], P('dp'), may hold values from 0.1 to 0.9
Outputs:
- hidden_input_gradient: bfloat16 [24576, 14336], P('dp', 'tensor')
- down_factor_gradient: float32 [14336, 128], P('tensor')
- up_factor_gradient: float32 [128, 4096], P(None, ('dp', 'tensor'))
- gate_gradient: float32 [24576, 2], P('dp')
The draws below stay inside these ranges and needn't reach their ends.
All inputs are finite; a program needn't handle non-finite values.
Results may differ from the reference program's by a relative error of at most 0.0031.
Values may be sent and summed in bfloat16 or wider, within the bound.
No kernel may reach another device: no remote copies, remote signals or barrier semaphores. Data moves between devices by JAX's collectives and lax.ppermute only.
A program may use at most 128 MiB of HBM per device.

```python
import jax
import jax.numpy as jnp
from jax import lax

OUTPUT_FEATURES = 4096
HIDDEN_UNITS = 14336
ADAPTER_EXPERTS = 8
LOW_RANK = 16
TOKENS = 24576


def raised(entries, stream_key, source, target, shards_of, factor):
    owner, partner = [(jnp.arange(entries.shape[dim]) // (entries.shape[dim] // shards_of)).reshape([-1 if axis == dim else 1 for axis in range(entries.ndim)]) for dim in (source, target)]
    chosen = jax.random.permutation(stream_key, shards_of)[partner]
    strong = (owner == chosen) | (owner == (partner + shards_of // 2) % shards_of)
    return jnp.where(strong, factor * entries, entries)


def block_scale(key, extent, pieces, low, high):
    gain, own = 1.0, jax.random.fold_in(key, 6)
    for dim, parts in pieces:
        draws = jnp.exp(jax.random.uniform(jax.random.fold_in(own, dim), (parts,), jnp.float32, low / len(pieces), high / len(pieces)))
        gain = gain * jnp.repeat(draws, extent[dim] // parts).reshape([-1 if axis == dim else 1 for axis in range(len(extent))])
    return gain


def distinct(rng, rows, number_of, top, lift):
    sequence = jax.random.permutation(jax.random.fold_in(rng, 1), number_of)
    boost = sequence
    for power in range(3):
        boost = boost * boost // number_of
    boost = boost * lift // number_of
    tickets = jax.random.randint(jax.random.fold_in(rng, 2), (rows, number_of), 0, 4096) + boost
    sure = jax.random.permutation(jax.random.fold_in(rng, 3), rows)[jnp.arange(number_of) % rows]
    tickets = jnp.where(jnp.arange(rows)[:, None] == sure[None, :], 1 << 14, tickets)
    merit = tickets * number_of + jnp.arange(number_of)
    return lax.top_k(merit.astype(jnp.int32), top)[1].astype(jnp.int32)


def gaussian(key, dims, width, bound, pieces=(), kind=jnp.bfloat16):
    gain = block_scale(key, dims, pieces, -0.22, 0.18) if pieces else 1.0
    entries = jax.random.normal(key, dims, jnp.float32) * width * gain
    return jnp.minimum(jnp.maximum(entries, -bound), bound).astype(kind)


def gaussian_with(own_key, dims, deviation, reach, split, heavy, kind=jnp.bfloat16):
    result = deviation * jax.random.normal(own_key, dims, jnp.float32)
    if split:
        result = result * block_scale(own_key, dims, split, -0.22, 0.18)
    return jnp.clip(raised(result, jax.random.fold_in(own_key, 3), *heavy), -reach, reach).astype(kind)


def setup_inputs(seed: int = 0) -> dict:
    keys = jax.random.split(jax.random.key(seed), 8)
    hidden = gaussian(keys[0], (TOKENS, HIDDEN_UNITS), 1.0, 6.0, ((0, 32), (1, 8)))
    layer_output_gradient = gaussian_with(keys[1], (TOKENS, OUTPUT_FEATURES), 1.0, 6.0, ((0, 32), (1, 8)), (0, 1, 32, 2.75))
    frozen_down_weight = gaussian(keys[2], (HIDDEN_UNITS, OUTPUT_FEATURES), HIDDEN_UNITS ** -0.5, 0.046875, ((0, 8), (1, 32)))
    adapter_down_weight = gaussian(keys[3], (HIDDEN_UNITS, ADAPTER_EXPERTS * LOW_RANK), HIDDEN_UNITS ** -0.5, 0.046875, ((0, 8),))
    adapter_up_weight = gaussian(keys[4], (ADAPTER_EXPERTS * LOW_RANK, OUTPUT_FEATURES), OUTPUT_FEATURES ** -0.5, 0.09375)
    chosen_expert_index = distinct(keys[5], TOKENS, ADAPTER_EXPERTS, 2, 2048)
    gates = jnp.clip(0.1 + 0.79999997 * jax.random.uniform(keys[6], (TOKENS, 2), jnp.float32) ** block_scale(keys[6], (TOKENS, 2), ((0, 32),), -0.2, 0.2), 0.1, 0.9)
    return {"hidden": hidden, "layer_output_gradient": layer_output_gradient, "frozen_down_weight": frozen_down_weight, "adapter_down_weight": adapter_down_weight, "adapter_up_weight": adapter_up_weight, "chosen_expert_index": chosen_expert_index, "gates": gates}


SCALE = 2.0


def reference(hidden, layer_output_gradient, frozen_down_weight, adapter_down_weight, adapter_up_weight, chosen_expert_index, gates):
    token_scale = float(TOKENS) ** -0.5
    rank_projection = jnp.dot(hidden, adapter_down_weight, preferred_element_type=jnp.float32)
    rank_output_gradient = lax.dot_general(layer_output_gradient, adapter_up_weight, (((1,), (1,)), ((), ())), preferred_element_type=jnp.float32)
    onehot = (chosen_expert_index[:, :, None] == jnp.arange(ADAPTER_EXPERTS, dtype=jnp.int32)[None, None, :]).astype(jnp.float32)
    weight = jnp.repeat(jnp.sum(onehot * gates[:, :, None], axis=1), LOW_RANK, axis=1)
    gated_rank_gradient = (SCALE * weight * rank_output_gradient).astype(jnp.bfloat16)
    gated_rank_projection = (SCALE * weight * rank_projection).astype(jnp.bfloat16)
    frozen_gradient_term = lax.dot_general(layer_output_gradient, frozen_down_weight, (((1,), (1,)), ((), ())), preferred_element_type=jnp.float32)
    adapter_gradient_term = lax.dot_general(gated_rank_gradient, adapter_down_weight, (((1,), (1,)), ((), ())), preferred_element_type=jnp.float32)
    hidden_input_gradient = (frozen_gradient_term + adapter_gradient_term).astype(jnp.bfloat16)
    down_factor_gradient = lax.dot_general(hidden, gated_rank_gradient, (((0,), (0,)), ((), ())), preferred_element_type=jnp.float32) * token_scale
    up_factor_gradient = lax.dot_general(gated_rank_projection, layer_output_gradient, (((0,), (0,)), ((), ())), preferred_element_type=jnp.float32) * token_scale
    product = jnp.sum((rank_projection * rank_output_gradient).reshape(rank_projection.shape[0], ADAPTER_EXPERTS, LOW_RANK), axis=2)
    gate_gradient = SCALE * jnp.sum(onehot * product[:, None, :], axis=2)
    return hidden_input_gradient, down_factor_gradient, up_factor_gradient, gate_gradient
```

```python
import functools

import jax
import jax.numpy as jnp
from jax import lax
from jax.experimental import pallas as pl
from jax.experimental.pallas import tpu as pltpu
from jax.sharding import PartitionSpec as P

EXPERTS = 8
RANK = 16
SCALE = 2.0
NZ, NY, NX = 8, 4, 4
ROWS_A = 1024
TILE = 256
Z_ORDER = (0, 1, -1, 2, -2, 3, -3, 4)
Z_GROUPS = [[z * NY + y for z in range(NZ)] for y in range(NY)]
VMEM_BYTES = 48 * 1024 * 1024


def move_z(value, step):
    pairs = [(z * NY + y, (z + step) % NZ * NY + y) for z in range(NZ) for y in range(NY)]
    return lax.ppermute(value, "dp", pairs)


def move_y(value, step):
    pairs = [(z * NY + y, z * NY + (y + step) % NY) for z in range(NZ) for y in range(NY)]
    return lax.ppermute(value, "dp", pairs)


def move_x(value, step):
    pairs = [(x * 2 + c, (x + step) % NX * 2 + c) for x in range(NX) for c in range(2)]
    return lax.ppermute(value, "tensor", pairs)


def swap_x(value, partner):
    return lax.ppermute(value, "tensor", [(x * 2 + c, partner(x) * 2 + c) for x in range(NX) for c in range(2)])


def swap_core(value):
    return lax.ppermute(value, "tensor", [(i, i ^ 1) for i in range(2 * NX)])


def arrange_kernel(place, near, far, out):
    z, y, x, c = place[0], place[1], place[2], place[3]
    for k, dz in enumerate(Z_ORDER):
        owner = lax.rem(z - dz + NZ, NZ)
        dx = lax.rem(x - lax.div(owner, 2) + NX, NX)
        same = lax.rem(owner, 2) == c
        for j in range(NY):
            lanes = pl.ds(pl.multiple_of(lax.rem(y - j + NY, NY) * 128, 128), 128)
            at = pl.ds((k * NY + j) * 128, 128)

            @pl.when(same)
            def _():
                out[:, at] = near[dx, :, lanes]

            @pl.when(jnp.logical_not(same))
            def _():
                out[:, at] = far[dx, :, lanes]


def arrange(place, near, far):
    tokens = near.shape[1]
    return pl.pallas_call(
        arrange_kernel,
        out_shape=jax.ShapeDtypeStruct((tokens, 4096), jnp.bfloat16),
        in_specs=[
            pl.BlockSpec(memory_space=pltpu.SMEM),
            pl.BlockSpec(memory_space=pltpu.VMEM),
            pl.BlockSpec(memory_space=pltpu.VMEM),
        ],
        out_specs=pl.BlockSpec(memory_space=pltpu.VMEM),
        compiler_params=pltpu.CompilerParams(vmem_limit_bytes=VMEM_BYTES),
        cost_estimate=pl.CostEstimate(flops=0, bytes_accessed=4 * tokens * 4096, transcendentals=0),
    )(place, near, far)


def finish(left, routed, right, factor):
    dims = (((1,), (1,)), ((), ()))
    total = lax.dot_general(left[...], right, dims, preferred_element_type=jnp.float32)
    total += lax.dot_general(routed[...], factor[...], dims, preferred_element_type=jnp.float32)
    return total.astype(jnp.bfloat16)


def kernel_a(left, routed, factor, n1, n2, p1, p2, m1, m2, fp1, fp2, fm1, fm2, out):
    low = pl.program_id(0) < 2
    parts = []
    for k in range(NZ):
        i = k if k < 3 else k - 3
        n, p, m, fp, fm = (n1, p1, m1, fp1, fm1) if k < 3 else (n2, p2, m2, fp2, fm2)
        parts += [n[i], p[i], jnp.where(low, fp[i], fm[i]), m[i]]
    out[...] = finish(left, routed, jnp.concatenate(parts, axis=1), factor)


def kernel_b(place, left, routed, factor, blocks, base, out):
    del base
    z = place[0]
    parts = []
    for dz in Z_ORDER:
        owner = lax.rem(z - dz + NZ, NZ)
        parts += [blocks[owner, j] for j in range(NY)]
    out[...] = finish(left, routed, jnp.concatenate(parts, axis=1), factor)


def cost(tokens, columns):
    return pl.CostEstimate(
        flops=2 * tokens * columns * 4224,
        bytes_accessed=2 * (tokens * 4224 + columns * 4224 + tokens * columns),
        transcendentals=0,
    )


def whole(shape):
    return pl.BlockSpec(shape, lambda n: (0,) * len(shape), pipeline_mode=pl.Buffered(1))


def project(place, left, routed, factor, a_blocks, b_blocks):
    tokens, depth = left.shape
    units = factor.shape[0]
    a_tiles = ROWS_A // TILE
    b_tiles = (units - ROWS_A) // TILE
    common = [whole((tokens, depth)), whole((tokens, 128))]
    a_specs = []
    for i, block in enumerate(a_blocks):
        if i < 6:
            index = lambda n: (0, n, 0)
        elif i < 8:
            index = lambda n: (0, jnp.minimum(n, 1), 0)
        else:
            index = lambda n: (0, jnp.maximum(n - 2, 0), 0)
        a_specs.append(pl.BlockSpec((block.shape[0], TILE, 128), index))
    params = pltpu.CompilerParams(vmem_limit_bytes=VMEM_BYTES)
    out_shape = jax.ShapeDtypeStruct((tokens, units), jnp.bfloat16)
    first = pl.pallas_call(
        kernel_a,
        grid=(a_tiles,),
        out_shape=out_shape,
        in_specs=common + [pl.BlockSpec((TILE, 128), lambda n: (n, 0))] + a_specs,
        out_specs=pl.BlockSpec((tokens, TILE), lambda n: (0, n)),
        compiler_params=params,
        cost_estimate=cost(tokens, ROWS_A),
    )(left, routed, factor, *a_blocks)
    return pl.pallas_call(
        kernel_b,
        grid=(b_tiles,),
        out_shape=out_shape,
        in_specs=[pl.BlockSpec(memory_space=pltpu.SMEM)]
        + common
        + [
            pl.BlockSpec((TILE, 128), lambda n: (n + a_tiles, 0)),
            pl.BlockSpec((NZ, NY, TILE, 128), lambda n: (0, 0, n, 0)),
            pl.BlockSpec(memory_space=pl.ANY),
        ],
        out_specs=pl.BlockSpec((tokens, TILE), lambda n: (0, n + a_tiles)),
        input_output_aliases={5: 0},
        compiler_params=params,
        cost_estimate=cost(tokens, units - ROWS_A),
    )(place, left, routed, factor, b_blocks, first)


def gather_a(own):
    half = own.shape[0] // 2
    up, down = [own], [own]
    for _ in range(3):
        up.append(move_z(up[-1], 1))
        down.append(move_z(down[-1], -1))
    across = jnp.concatenate([move_z(up[3][:half], 1), move_z(down[3][half:], -1)], axis=0)
    first = jnp.stack([own, up[1], down[1]])
    second = jnp.stack([up[2], down[2], up[3], down[3], across])
    blocks = [[first, second], [], [], [], []]
    for group in (first, second):
        plus = move_y(group, 1)
        minus = move_y(group, -1)
        blocks[1].append(plus)
        blocks[2].append(minus)
        blocks[3].append(move_y(plus[:, :half], 1))
        blocks[4].append(move_y(minus[:, half:], -1))
    return [piece for pair in blocks for piece in pair]


def gather_b(own):
    half = own.shape[0] // 2
    plus = move_y(own, 1)
    minus = move_y(own, -1)
    across = jnp.concatenate([move_y(plus[:half], 1), move_y(minus[half:], -1)], axis=0)
    column = jnp.stack([own, plus, across, minus])
    return lax.all_gather(column, "dp", axis=0, axis_index_groups=Z_GROUPS)


def gather_tokens(own):
    half = own.shape[0] // 2
    plus = move_x(own, 1)
    minus = move_x(own, -1)
    across = jnp.concatenate([move_x(plus[:half], 1), move_x(minus[half:], -1)], axis=0)
    near = jnp.stack([own, plus, across, minus])
    return near, swap_core(near)


def sum_tensor(value, core):
    half = value.shape[0] // 2
    halves = value.reshape(2, half, value.shape[1])
    kept = lax.dynamic_index_in_dim(halves, core, 0, keepdims=False)
    sent = lax.dynamic_index_in_dim(halves, 1 - core, 0, keepdims=False)
    kept = kept + swap_core(sent)
    kept = kept + swap_x(kept, lambda x: x ^ 1)
    kept = kept + swap_x(kept, lambda x: 3 - x)
    other = swap_core(kept)
    return jnp.where(core == 0, jnp.concatenate([kept, other]), jnp.concatenate([other, kept]))


def per_device(
    hidden,
    layer_output_gradient,
    frozen_down_weight,
    adapter_down_weight,
    adapter_up_weight,
    chosen_expert_index,
    gates,
):
    dp_index = lax.axis_index("dp").astype(jnp.int32)
    tensor_index = lax.axis_index("tensor").astype(jnp.int32)
    core = lax.rem(tensor_index, 2)
    place = jnp.stack([lax.div(dp_index, NY), lax.rem(dp_index, NY), lax.div(tensor_index, 2), core])
    tokens_here, width = layer_output_gradient.shape
    token_scale = float(tokens_here * NZ * NY) ** (-0.5)

    a_blocks = gather_a(frozen_down_weight[:ROWS_A])
    b_blocks = gather_b(frozen_down_weight[ROWS_A:])
    near, far = gather_tokens(layer_output_gradient)
    left = arrange(place, near, far)

    inner_part = jnp.dot(hidden, adapter_down_weight, preferred_element_type=jnp.float32)
    up_here = lax.dynamic_slice_in_dim(adapter_up_weight, tensor_index * width, width, axis=1)
    outer_part = lax.dot_general(
        layer_output_gradient, up_here, (((1,), (1,)), ((), ())), preferred_element_type=jnp.float32
    )
    both = sum_tensor(jnp.concatenate([inner_part, outer_part], axis=1), core)
    inner, outer = both[:, :128], both[:, 128:]
    onehot = (
        chosen_expert_index[:, :, None] == jnp.arange(EXPERTS, dtype=jnp.int32)[None, None, :]
    ).astype(jnp.float32)
    weight = jnp.repeat(jnp.sum(onehot * gates[:, :, None], axis=1), RANK, axis=1)
    routed_outer = (SCALE * weight * outer).astype(jnp.bfloat16)
    routed_inner = (SCALE * weight * inner).astype(jnp.bfloat16)
    product = jnp.sum((inner * outer).reshape(tokens_here, EXPERTS, RANK), axis=2)
    gate_gradient = SCALE * jnp.sum(onehot * product[:, None, :], axis=2)

    over_tokens = (((0,), (0,)), ((), ()))
    down_part = lax.dot_general(hidden, routed_outer, over_tokens, preferred_element_type=jnp.float32)
    up_part = lax.dot_general(
        layer_output_gradient, routed_inner, over_tokens, preferred_element_type=jnp.float32
    )
    n = NZ * NY
    parts = jnp.concatenate([down_part.reshape(n, -1, 128), up_part.reshape(n, -1, 128)], axis=1)
    parts = lax.all_to_all(parts.astype(jnp.bfloat16), "dp", 0, 0, tiled=True)
    total = jnp.sum(parts.astype(jnp.float32), axis=0) * token_scale
    down_rows = down_part.shape[0] // n
    down_factor_gradient = lax.all_gather(total[:down_rows], "dp", axis=0, tiled=True)
    pairs = [(d * 8 + t, (4 * t + d // 8) * 8 + d % 8) for d in range(n) for t in range(8)]
    up_factor_gradient = lax.ppermute(total[down_rows:], ("dp", "tensor"), pairs).T

    hidden_input_gradient = project(place, left, routed_outer, adapter_down_weight, a_blocks, b_blocks)
    return (hidden_input_gradient, down_factor_gradient, up_factor_gradient, gate_gradient)


def solution(mesh):
    return jax.shard_map(
        per_device,
        mesh=mesh,
        in_specs=(
            P("dp", "tensor"),
            P("dp", "tensor"),
            P("tensor", "dp"),
            P("tensor", None),
            P(),
            P("dp", None),
            P("dp", None),
        ),
        out_specs=(P("dp", "tensor"), P("tensor", None), P(None, ("dp", "tensor")), P("dp", None)),
        check_vma=False,
    )
```

```python
import jax
import jax.numpy as jnp
from jax import lax
from jax.experimental import pallas as pl
from jax.experimental.pallas import tpu as pltpu
from jax.sharding import PartitionSpec as P

EXPERTS = 8
RANK = 16
SCALE = 2.0
NZ, NY, NX = 8, 4, 4
ROWS_A = 1024
TILE = 256
Z_GROUPS = [[z * NY + y for z in range(NZ)] for y in range(NY)]
VMEM_BYTES = 60 * 1024 * 1024
LAST = (((1,), (1,)), ((), ()))
FIRST = (((0,), (0,)), ((), ()))


def move_y(value, step):
    pairs = [(z * NY + y, z * NY + (y + step) % NY) for z in range(NZ) for y in range(NY)]
    return lax.ppermute(value, "dp", pairs)


def turn_x(value):
    pairs = [(x * 2 + c, (x + 1 - 2 * c) % NX * 2 + c) for x in range(NX) for c in range(2)]
    return lax.ppermute(value, "tensor", pairs)


def swap_x(value, partner):
    return lax.ppermute(value, "tensor", [(x * 2 + c, partner(x) * 2 + c) for x in range(NX) for c in range(2)])


def swap_core(value):
    return lax.ppermute(value, "tensor", [(i, i ^ 1) for i in range(2 * NX)])


def full(*shape):
    return pl.BlockSpec(shape, lambda n: (0,) * len(shape))


def smem():
    return pl.BlockSpec(memory_space=pltpu.SMEM)


PARAMS = pltpu.CompilerParams(vmem_limit_bytes=VMEM_BYTES)
LIGHT = pl.CostEstimate(flops=0, bytes_accessed=0, transcendentals=0)


def project_low_rank_kernel(place, hidden, factor, gradient, up, kept, sent):
    half = kept.shape[0]
    width = gradient.shape[1]
    tensor = place[2] * 2 + place[3]
    lanes = pl.ds(pl.multiple_of(tensor * width, width), width)
    mine = pl.ds(pl.multiple_of(place[3] * half, half), half)
    other = pl.ds(pl.multiple_of((1 - place[3]) * half, half), half)
    for rows, out in ((mine, kept), (other, sent)):
        out[:, :128] = jnp.dot(hidden[rows, :], factor[...], preferred_element_type=jnp.float32)
        out[:, 128:] = lax.dot_general(
            gradient[rows, :], up[:, lanes], LAST, preferred_element_type=jnp.float32
        )


def project_low_rank(place, hidden, factor, gradient, up):
    half = jax.ShapeDtypeStruct((hidden.shape[0] // 2, 256), jnp.float32)
    return pl.pallas_call(
        project_low_rank_kernel,
        grid=(1,),
        out_shape=(half, half),
        in_specs=[smem()] + [full(*value.shape) for value in (hidden, factor, gradient, up)],
        out_specs=(full(*half.shape), full(*half.shape)),
        compiler_params=PARAMS,
        cost_estimate=LIGHT,
    )(place, hidden, factor, gradient, up)


def route_kernel(place, kept, other, chosen, gates, hidden, gradient, *refs):
    chunks, (routed, gate_gradient, parts) = refs[:NY], refs[NY:]
    zero = place[3] == 0
    both = jnp.concatenate(
        [jnp.where(zero, kept[...], other[...]), jnp.where(zero, other[...], kept[...])], axis=0
    )
    inner, outer = both[:, :128], both[:, 128:]
    expert = lax.broadcasted_iota(jnp.int32, inner.shape, 1) // RANK
    hits = [chosen[:, k : k + 1] == expert for k in range(2)]
    weight = jnp.where(hits[0], gates[:, 0:1], 0.0) + jnp.where(hits[1], gates[:, 1:2], 0.0)
    routed_outer = (SCALE * weight * outer).astype(jnp.bfloat16)
    routed_inner = (SCALE * weight * inner).astype(jnp.bfloat16)
    routed[...] = routed_outer
    product = inner * outer
    for k in range(2):
        picked = jnp.where(hits[k], product, 0.0)
        gate_gradient[:, k : k + 1] = SCALE * jnp.sum(picked, axis=1, keepdims=True)
    down = lax.dot_general(hidden[...], routed_outer, FIRST, preferred_element_type=jnp.float32)
    up = lax.dot_general(gradient[...], routed_inner, FIRST, preferred_element_type=jnp.float32)
    n = NZ * NY
    for whole_sum, first in ((down, 0), (up, down.shape[0] // n)):
        rows = whole_sum.shape[0] // n
        pieces = whole_sum.astype(jnp.bfloat16).reshape(NZ, NY, rows, 128)
        for y in range(NY):
            parts[y, :, pl.ds(first, rows), :] = pieces[:, y]
    for j, chunk in enumerate(chunks):
        chunk[...] = parts[lax.rem(place[1] + j, NY)]


def route(place, kept, other, chosen, gates, hidden, gradient):
    n = NZ * NY
    tokens = hidden.shape[0]
    rows = (hidden.shape[1] + gradient.shape[1]) // n
    outs = (
        *[jax.ShapeDtypeStruct((NZ, rows, 128), jnp.bfloat16)] * NY,
        jax.ShapeDtypeStruct((tokens, 128), jnp.bfloat16),
        jax.ShapeDtypeStruct((tokens, 2), jnp.float32),
    )
    return pl.pallas_call(
        route_kernel,
        grid=(1,),
        out_shape=outs,
        in_specs=[smem()]
        + [full(*value.shape) for value in (kept, other, chosen, gates, hidden, gradient)],
        out_specs=tuple(full(*out.shape) for out in outs),
        scratch_shapes=[pltpu.VMEM((NY, NZ, rows, 128), jnp.bfloat16)],
        compiler_params=PARAMS,
        cost_estimate=LIGHT,
    )(place, kept, other, chosen, gates, hidden, gradient)


def copied(*values):
    def kernel(*refs):
        for i in range(len(values)):
            refs[len(values) + i][...] = refs[i][...]

    specs = [full(*value.shape) for value in values]
    return pl.pallas_call(
        kernel,
        grid=(1,),
        out_shape=tuple(jax.ShapeDtypeStruct(value.shape, value.dtype) for value in values),
        in_specs=specs,
        out_specs=tuple(specs),
        compiler_params=PARAMS,
        cost_estimate=LIGHT,
    )(*values)


def arrange_kernel(place, *refs):
    out = refs[-1]
    x, c = place[2], place[3]
    sign = 1 - 2 * c
    width = out.shape[1] // 8
    for step in range(NX):
        for block, turn, core in ((refs[step], sign, c), (refs[NX + step], -sign, 1 - c)):
            owner = lax.rem(x - turn * step + 2 * NX, NX) * 2 + core
            out[:, pl.ds(pl.multiple_of(owner * width, width), width)] = block[...]


def arrange(place, blocks):
    tokens, width = blocks[0].shape
    return pl.pallas_call(
        arrange_kernel,
        grid=(1,),
        out_shape=jax.ShapeDtypeStruct((tokens, width * 8), jnp.bfloat16),
        in_specs=[smem()] + [full(*block.shape) for block in blocks],
        out_specs=full(tokens, width * 8),
        compiler_params=PARAMS,
        cost_estimate=LIGHT,
    )(place, *blocks)


A_TILES = ROWS_A // TILE


A_TILES = ROWS_A // TILE


def lanes_of(place, z, dy):
    owner = z * NY + lax.rem(place[1] - dy + NY, NY)
    return pl.ds(pl.multiple_of(owner * 128, 128), 128)


def own_kernel(place, left, routed, factor, own, out, sides, later, picked):
    @pl.when(pl.program_id(0) == 0)
    def _():
        for z in range(NZ):
            lanes = pl.ds(z * 128, 128)
            picked[:, lanes] = left[:, lanes_of(place, z, 0)]
            sides[:, lanes] = left[:, lanes_of(place, z, 1)]
            sides[:, pl.ds((NZ + z) * 128, 128)] = left[:, lanes_of(place, z, -1)]
            later[:, lanes] = left[:, lanes_of(place, z, 2)]

    right = jnp.concatenate([own[z] for z in range(NZ)], axis=1)
    total = lax.dot_general(picked[...], right, LAST, preferred_element_type=jnp.float32)
    total += lax.dot_general(routed[...], factor[...], LAST, preferred_element_type=jnp.float32)
    out[...] = total


def sides_kernel(picked, partial, plus, minus, out):
    right = jnp.concatenate([side[z] for side in (plus, minus) for z in range(NZ)], axis=1)
    total = lax.dot_general(picked[...], right, LAST, preferred_element_type=jnp.float32)
    out[...] = total + partial[...]


def last_rows_kernel(place, left, routed, factor, blocks, out, right):
    for z in range(NZ):
        for dy in range(NY):
            right[:, lanes_of(place, z, dy)] = blocks[z, dy]
    total = lax.dot_general(left[...], right[...], LAST, preferred_element_type=jnp.float32)
    total += lax.dot_general(routed[...], factor[...], LAST, preferred_element_type=jnp.float32)
    out[...] = total.astype(out.dtype)


def late_kernel(picked, partial, low, high, base, out):
    del base
    blocks = [low[z] for z in range(NZ // 2)] + [high[z] for z in range(NZ // 2)]
    right = jnp.concatenate(blocks, axis=1)
    total = lax.dot_general(picked[...], right, LAST, preferred_element_type=jnp.float32)
    out[...] = (total + partial[...]).astype(out.dtype)


def whole(shape):
    return pl.BlockSpec(shape, lambda n: (0,) * len(shape), pipeline_mode=pl.Buffered(1))


def project_own(place, left, routed, factor, own):
    tokens, depth = left.shape
    used = depth // NY
    return pl.pallas_call(
        own_kernel,
        grid=(A_TILES,),
        out_shape=(
            jax.ShapeDtypeStruct((tokens, ROWS_A), jnp.float32),
            jax.ShapeDtypeStruct((tokens, 2 * used), jnp.bfloat16),
            jax.ShapeDtypeStruct((tokens, used), jnp.bfloat16),
        ),
        in_specs=[smem(), whole((tokens, depth)), whole((tokens, 128))]
        + [pl.BlockSpec((TILE, 128), lambda n: (n, 0))]
        + [pl.BlockSpec((NZ, TILE, 128), lambda n: (0, n, 0))],
        out_specs=(
            pl.BlockSpec((tokens, TILE), lambda n: (0, n)),
            pl.BlockSpec((tokens, 2 * used), lambda n: (0, 0)),
            pl.BlockSpec((tokens, used), lambda n: (0, 0)),
        ),
        scratch_shapes=[pltpu.VMEM((tokens, used), jnp.bfloat16)],
        compiler_params=PARAMS,
        cost_estimate=LIGHT,
    )(place, left, routed, factor, own)


def project_sides(picked, partial, plus, minus):
    tokens, depth = picked.shape
    return pl.pallas_call(
        sides_kernel,
        grid=(A_TILES,),
        out_shape=jax.ShapeDtypeStruct(partial.shape, jnp.float32),
        in_specs=[whole((tokens, depth)), pl.BlockSpec((tokens, TILE), lambda n: (0, n))]
        + [pl.BlockSpec((NZ, TILE, 128), lambda n: (0, n, 0))] * 2,
        out_specs=pl.BlockSpec((tokens, TILE), lambda n: (0, n)),
        compiler_params=PARAMS,
        cost_estimate=LIGHT,
    )(picked, partial, plus, minus)


def project_last_rows(place, left, routed, factor, blocks):
    tokens, depth = left.shape
    units = factor.shape[0]
    return pl.pallas_call(
        last_rows_kernel,
        grid=(units // TILE - A_TILES,),
        out_shape=jax.ShapeDtypeStruct((tokens, units), jnp.bfloat16),
        in_specs=[smem(), whole((tokens, depth)), whole((tokens, 128))]
        + [
            pl.BlockSpec((TILE, 128), lambda n: (n + A_TILES, 0)),
            pl.BlockSpec((NZ, NY, TILE, 128), lambda n: (0, 0, n, 0)),
        ],
        out_specs=pl.BlockSpec((tokens, TILE), lambda n: (0, n + A_TILES)),
        scratch_shapes=[pltpu.VMEM((TILE, depth), jnp.bfloat16)],
        compiler_params=PARAMS,
        cost_estimate=LIGHT,
    )(place, left, routed, factor, blocks)


def project_late(picked, partial, low, high, base):
    tokens, depth = picked.shape
    return pl.pallas_call(
        late_kernel,
        grid=(A_TILES,),
        out_shape=jax.ShapeDtypeStruct(base.shape, jnp.bfloat16),
        in_specs=[whole((tokens, depth)), pl.BlockSpec((tokens, TILE), lambda n: (0, n))]
        + [pl.BlockSpec((NZ // 2, TILE, 128), lambda n: (0, n, 0))] * 2
        + [pl.BlockSpec(memory_space=pl.ANY)],
        out_specs=pl.BlockSpec((tokens, TILE), lambda n: (0, n)),
        input_output_aliases={4: 0},
        compiler_params=PARAMS,
        cost_estimate=LIGHT,
    )(picked, partial, low, high, base)


def per_device(
    hidden,
    layer_output_gradient,
    frozen_down_weight,
    adapter_down_weight,
    adapter_up_weight,
    chosen_expert_index,
    gates,
):
    together = lambda *values: lax.optimization_barrier(values)
    dp_index = lax.axis_index("dp").astype(jnp.int32)
    tensor_index = lax.axis_index("tensor").astype(jnp.int32)
    place = jnp.stack(
        [lax.div(dp_index, NY), lax.rem(dp_index, NY), lax.div(tensor_index, 2), lax.rem(tensor_index, 2)]
    )
    tokens_here = hidden.shape[0]
    token_scale = float(tokens_here * NZ * NY) ** (-0.5)
    n = NZ * NY

    own, last = frozen_down_weight[:ROWS_A], frozen_down_weight[ROWS_A:]
    row = lax.all_gather(own, "dp", axis=0, axis_index_groups=Z_GROUPS)
    kept, sent = project_low_rank(
        place, hidden, adapter_down_weight, layer_output_gradient, adapter_up_weight
    )
    last, kept, sent = together(last, kept, sent)
    b1, b2, b3 = move_y(last, 1), move_y(last, 2), move_y(last, -1)
    near = [layer_output_gradient, turn_x(layer_output_gradient)]
    kept = kept + swap_core(sent)
    kept = kept + swap_x(kept, lambda x: x ^ 1)
    chosen, weights = copied(chosen_expert_index, gates)
    kept, chosen, weights = together(kept, chosen, weights)
    kept = kept + swap_x(kept, lambda x: 3 - x)
    b1, b2, b3, kept, near[1] = together(b1, b2, b3, kept, near[1])
    column = jnp.stack([last, b1, b2, b3])
    b_blocks = lax.all_gather(column, "dp", axis=0, axis_index_groups=Z_GROUPS)

    other = swap_core(kept)
    *chunks, routed, gate_gradient = route(
        place, kept, other, chosen, weights, hidden, layer_output_gradient
    )
    near.append(turn_x(near[-1]))

    came = [move_y(chunks[j], j) for j in range(1, NY)]
    parts = sum(chunk.astype(jnp.float32) for chunk in [chunks[0]] + came).astype(jnp.bfloat16)
    row, parts, near[2] = together(row, parts, near[2])
    plus, minus = move_y(row, 1), move_y(row, -1)
    parts = lax.all_to_all(parts, "dp", 0, 0, tiled=True, axis_index_groups=Z_GROUPS)
    total = jnp.sum(parts.astype(jnp.float32), axis=0) * token_scale
    down_rows = hidden.shape[1] // n
    down = jnp.broadcast_to(total[:down_rows].astype(jnp.bfloat16)[None], (NZ, down_rows, 128))
    down = lax.all_to_all(down, "dp", 0, 0, tiled=True, axis_index_groups=Z_GROUPS)
    near.append(turn_x(near[-1]))
    left = arrange(place, near + [swap_core(block) for block in near])
    partial, side_left, late_left = project_own(place, left, routed, adapter_down_weight, row)
    came = [down] + [move_y(down, j) for j in range(1, NY)]
    plus, minus, partial, side_left, late_left, *came = together(
        plus, minus, partial, side_left, late_left, *came
    )

    half = NZ // 2
    low, high = move_y(plus[:half], 1), move_y(minus[half:], -1)
    partial = project_sides(side_left, partial, plus, minus)
    pairs = [(d * 8 + t, (4 * t + d // 8) * 8 + d % 8) for d in range(n) for t in range(8)]
    up_factor_gradient = lax.ppermute(total[down_rows:], ("dp", "tensor"), pairs).T
    came = jnp.stack([came[(3 - i) % NY] for i in range(2 * NY - 1)])
    came = lax.dynamic_slice_in_dim(came, 3 - place[1], NY, axis=0)
    down_factor_gradient = came.transpose(1, 0, 2, 3).reshape(-1, 128).astype(jnp.float32)

    hidden_input_gradient = project_last_rows(place, left, routed, adapter_down_weight, b_blocks)
    hidden_input_gradient, low, high, partial, down_factor_gradient, up_factor_gradient = together(
        hidden_input_gradient, low, high, partial, down_factor_gradient, up_factor_gradient
    )
    hidden_input_gradient = project_late(late_left, partial, low, high, hidden_input_gradient)
    return (hidden_input_gradient, down_factor_gradient, up_factor_gradient, gate_gradient)


def solution(mesh):
    return jax.shard_map(
        per_device,
        mesh=mesh,
        in_specs=(
            P("dp", "tensor"),
            P("dp", "tensor"),
            P("tensor", "dp"),
            P("tensor", None),
            P(),
            P("dp", None),
            P("dp", None),
        ),
        out_specs=(P("dp", "tensor"), P("tensor", None), P(None, ("dp", "tensor")), P("dp", None)),
        check_vma=False,
    )
```

```python
import jax
import jax.numpy as jnp
from jax import lax
from jax.experimental import pallas as pl
from jax.experimental.pallas import tpu as pltpu
from jax.sharding import PartitionSpec as P

EXPERTS = 8
RANK = 16
SCALE = 2.0
NZ, NY, NX = 8, 4, 4
ROWS_A = 1024
TILE = 256
Z_GROUPS = [[z * NY + y for z in range(NZ)] for y in range(NY)]
VMEM_BYTES = 60 * 1024 * 1024
LAST = (((1,), (1,)), ((), ()))
FIRST = (((0,), (0,)), ((), ()))


def move_y(value, step):
    pairs = [(z * NY + y, z * NY + (y + step) % NY) for z in range(NZ) for y in range(NY)]
    return lax.ppermute(value, "dp", pairs)


def turn_x(value):
    pairs = [(x * 2 + c, (x + 1 - 2 * c) % NX * 2 + c) for x in range(NX) for c in range(2)]
    return lax.ppermute(value, "tensor", pairs)


def swap_x(value, partner):
    return lax.ppermute(value, "tensor", [(x * 2 + c, partner(x) * 2 + c) for x in range(NX) for c in range(2)])


def swap_core(value):
    return lax.ppermute(value, "tensor", [(i, i ^ 1) for i in range(2 * NX)])


def full(*shape):
    return pl.BlockSpec(shape, lambda n: (0,) * len(shape))


def smem():
    return pl.BlockSpec(memory_space=pltpu.SMEM)


PARAMS = pltpu.CompilerParams(vmem_limit_bytes=VMEM_BYTES)
LIGHT = pl.CostEstimate(flops=0, bytes_accessed=0, transcendentals=0)


def project_low_rank_kernel(place, hidden, factor, gradient, up, kept, sent):
    half = kept.shape[0]
    width = gradient.shape[1]
    tensor = place[2] * 2 + place[3]
    lanes = pl.ds(pl.multiple_of(tensor * width, width), width)
    mine = pl.ds(pl.multiple_of(place[3] * half, half), half)
    other = pl.ds(pl.multiple_of((1 - place[3]) * half, half), half)
    for rows, out in ((mine, kept), (other, sent)):
        out[:, :128] = jnp.dot(hidden[rows, :], factor[...], preferred_element_type=jnp.float32)
        out[:, 128:] = lax.dot_general(
            gradient[rows, :], up[:, lanes], LAST, preferred_element_type=jnp.float32
        )


def project_low_rank(place, hidden, factor, gradient, up):
    half = jax.ShapeDtypeStruct((hidden.shape[0] // 2, 256), jnp.float32)
    return pl.pallas_call(
        project_low_rank_kernel,
        grid=(1,),
        out_shape=(half, half),
        in_specs=[smem()] + [full(*value.shape) for value in (hidden, factor, gradient, up)],
        out_specs=(full(*half.shape), full(*half.shape)),
        compiler_params=PARAMS,
        cost_estimate=LIGHT,
    )(place, hidden, factor, gradient, up)


def route_kernel(place, kept, other, chosen, gates, hidden, gradient, *refs):
    chunks, (routed, gate_gradient, parts) = refs[:NY], refs[NY:]
    zero = place[3] == 0
    both = jnp.concatenate(
        [jnp.where(zero, kept[...], other[...]), jnp.where(zero, other[...], kept[...])], axis=0
    )
    inner, outer = both[:, :128], both[:, 128:]
    expert = lax.broadcasted_iota(jnp.int32, inner.shape, 1) // RANK
    hits = [chosen[:, k : k + 1] == expert for k in range(2)]
    weight = jnp.where(hits[0], gates[:, 0:1], 0.0) + jnp.where(hits[1], gates[:, 1:2], 0.0)
    routed_outer = (SCALE * weight * outer).astype(jnp.bfloat16)
    routed_inner = (SCALE * weight * inner).astype(jnp.bfloat16)
    routed[...] = routed_outer
    product = inner * outer
    for k in range(2):
        picked = jnp.where(hits[k], product, 0.0)
        gate_gradient[:, k : k + 1] = SCALE * jnp.sum(picked, axis=1, keepdims=True)
    down = lax.dot_general(hidden[...], routed_outer, FIRST, preferred_element_type=jnp.float32)
    up = lax.dot_general(gradient[...], routed_inner, FIRST, preferred_element_type=jnp.float32)
    n = NZ * NY
    for whole_sum, first in ((down, 0), (up, down.shape[0] // n)):
        rows = whole_sum.shape[0] // n
        pieces = whole_sum.astype(jnp.bfloat16).reshape(NZ, NY, rows, 128)
        for y in range(NY):
            parts[y, :, pl.ds(first, rows), :] = pieces[:, y]
    for j, chunk in enumerate(chunks):
        chunk[...] = parts[lax.rem(place[1] + j, NY)]


def route(place, kept, other, chosen, gates, hidden, gradient):
    n = NZ * NY
    tokens = hidden.shape[0]
    rows = (hidden.shape[1] + gradient.shape[1]) // n
    outs = (
        *[jax.ShapeDtypeStruct((NZ, rows, 128), jnp.bfloat16)] * NY,
        jax.ShapeDtypeStruct((tokens, 128), jnp.bfloat16),
        jax.ShapeDtypeStruct((tokens, 2), jnp.float32),
    )
    return pl.pallas_call(
        route_kernel,
        grid=(1,),
        out_shape=outs,
        in_specs=[smem()]
        + [full(*value.shape) for value in (kept, other, chosen, gates, hidden, gradient)],
        out_specs=tuple(full(*out.shape) for out in outs),
        scratch_shapes=[pltpu.VMEM((NY, NZ, rows, 128), jnp.bfloat16)],
        compiler_params=PARAMS,
        cost_estimate=LIGHT,
    )(place, kept, other, chosen, gates, hidden, gradient)


def copied(*values):
    def kernel(*refs):
        for i in range(len(values)):
            refs[len(values) + i][...] = refs[i][...]

    specs = [full(*value.shape) for value in values]
    return pl.pallas_call(
        kernel,
        grid=(1,),
        out_shape=tuple(jax.ShapeDtypeStruct(value.shape, value.dtype) for value in values),
        in_specs=specs,
        out_specs=tuple(specs),
        compiler_params=PARAMS,
        cost_estimate=LIGHT,
    )(*values)


def arrange_kernel(place, *refs):
    out = refs[-1]
    x, c = place[2], place[3]
    sign = 1 - 2 * c
    width = out.shape[1] // 8
    for step in range(NX):
        for block, turn, core in ((refs[step], sign, c), (refs[NX + step], -sign, 1 - c)):
            owner = lax.rem(x - turn * step + 2 * NX, NX) * 2 + core
            out[:, pl.ds(pl.multiple_of(owner * width, width), width)] = block[...]


def arrange(place, blocks):
    tokens, width = blocks[0].shape
    return pl.pallas_call(
        arrange_kernel,
        grid=(1,),
        out_shape=jax.ShapeDtypeStruct((tokens, width * 8), jnp.bfloat16),
        in_specs=[smem()] + [full(*block.shape) for block in blocks],
        out_specs=full(tokens, width * 8),
        compiler_params=PARAMS,
        cost_estimate=LIGHT,
    )(place, *blocks)


A_TILES = ROWS_A // TILE


A_TILES = ROWS_A // TILE


def lanes_of(place, z, dy):
    owner = z * NY + lax.rem(place[1] - dy + NY, NY)
    return pl.ds(pl.multiple_of(owner * 128, 128), 128)


def early_kernel(place, left, routed, factor, own, p0, p1, m0, m1, out, later, right, picked):
    half = NZ // 2

    @pl.when(pl.program_id(0) == 0)
    def _():
        for z in range(NZ):
            for s, dy in enumerate((0, 1, -1)):
                picked[:, pl.ds((s * NZ + z) * 128, 128)] = left[:, lanes_of(place, z, dy)]
            later[:, pl.ds(z * 128, 128)] = left[:, lanes_of(place, z, 2)]

    for s, pair in enumerate(((own, own), (p0, p1), (m0, m1))):
        for z in range(NZ):
            ref, i = pair[z // half], z if s == 0 else z % half
            right[:, pl.ds((s * NZ + z) * 128, 128)] = ref[i]
    total = lax.dot_general(picked[...], right[...], LAST, preferred_element_type=jnp.float32)
    total += lax.dot_general(routed[...], factor[...], LAST, preferred_element_type=jnp.float32)
    out[...] = total


def last_rows_kernel(place, left, routed, factor, blocks, out, right):
    for z in range(NZ):
        for dy in range(NY):
            right[:, lanes_of(place, z, dy)] = blocks[z, dy]
    total = lax.dot_general(left[...], right[...], LAST, preferred_element_type=jnp.float32)
    total += lax.dot_general(routed[...], factor[...], LAST, preferred_element_type=jnp.float32)
    out[...] = total.astype(out.dtype)


def late_kernel(picked, partial, low, high, base, out):
    del base
    blocks = [low[z] for z in range(NZ // 2)] + [high[z] for z in range(NZ // 2)]
    right = jnp.concatenate(blocks, axis=1)
    total = lax.dot_general(picked[...], right, LAST, preferred_element_type=jnp.float32)
    out[...] = (total + partial[...]).astype(out.dtype)


def whole(shape):
    return pl.BlockSpec(shape, lambda n: (0,) * len(shape), pipeline_mode=pl.Buffered(1))


def project_early(place, left, routed, factor, own, *sides):
    tokens, depth = left.shape
    used = 3 * depth // NY
    return pl.pallas_call(
        early_kernel,
        grid=(A_TILES,),
        out_shape=(
            jax.ShapeDtypeStruct((tokens, ROWS_A), jnp.float32),
            jax.ShapeDtypeStruct((tokens, depth - used), jnp.bfloat16),
        ),
        in_specs=[smem(), whole((tokens, depth)), whole((tokens, 128))]
        + [pl.BlockSpec((TILE, 128), lambda n: (n, 0))]
        + [pl.BlockSpec((NZ, TILE, 128), lambda n: (0, n, 0))]
        + [pl.BlockSpec((NZ // 2, TILE, 128), lambda n: (0, n, 0))] * 4,
        out_specs=(
            pl.BlockSpec((tokens, TILE), lambda n: (0, n)),
            pl.BlockSpec((tokens, depth - used), lambda n: (0, 0)),
        ),
        scratch_shapes=[pltpu.VMEM((TILE, used), jnp.bfloat16), pltpu.VMEM((tokens, used), jnp.bfloat16)],
        compiler_params=PARAMS,
        cost_estimate=LIGHT,
    )(place, left, routed, factor, own, *sides)


def project_last_rows(place, left, routed, factor, blocks):
    tokens, depth = left.shape
    units = factor.shape[0]
    return pl.pallas_call(
        last_rows_kernel,
        grid=(units // TILE - A_TILES,),
        out_shape=jax.ShapeDtypeStruct((tokens, units), jnp.bfloat16),
        in_specs=[smem(), whole((tokens, depth)), whole((tokens, 128))]
        + [
            pl.BlockSpec((TILE, 128), lambda n: (n + A_TILES, 0)),
            pl.BlockSpec((NZ, NY, TILE, 128), lambda n: (0, 0, n, 0)),
        ],
        out_specs=pl.BlockSpec((tokens, TILE), lambda n: (0, n + A_TILES)),
        scratch_shapes=[pltpu.VMEM((TILE, depth), jnp.bfloat16)],
        compiler_params=PARAMS,
        cost_estimate=LIGHT,
    )(place, left, routed, factor, blocks)


def project_late(picked, partial, low, high, base):
    tokens, depth = picked.shape
    return pl.pallas_call(
        late_kernel,
        grid=(A_TILES,),
        out_shape=jax.ShapeDtypeStruct(base.shape, jnp.bfloat16),
        in_specs=[whole((tokens, depth)), pl.BlockSpec((tokens, TILE), lambda n: (0, n))]
        + [pl.BlockSpec((NZ // 2, TILE, 128), lambda n: (0, n, 0))] * 2
        + [pl.BlockSpec(memory_space=pl.ANY)],
        out_specs=pl.BlockSpec((tokens, TILE), lambda n: (0, n)),
        input_output_aliases={4: 0},
        compiler_params=PARAMS,
        cost_estimate=LIGHT,
    )(picked, partial, low, high, base)


def per_device(
    hidden,
    layer_output_gradient,
    frozen_down_weight,
    adapter_down_weight,
    adapter_up_weight,
    chosen_expert_index,
    gates,
):
    together = lambda *values: lax.optimization_barrier(values)
    dp_index = lax.axis_index("dp").astype(jnp.int32)
    tensor_index = lax.axis_index("tensor").astype(jnp.int32)
    place = jnp.stack(
        [lax.div(dp_index, NY), lax.rem(dp_index, NY), lax.div(tensor_index, 2), lax.rem(tensor_index, 2)]
    )
    tokens_here = hidden.shape[0]
    token_scale = float(tokens_here * NZ * NY) ** (-0.5)
    n = NZ * NY

    own, last = frozen_down_weight[:ROWS_A], frozen_down_weight[ROWS_A:]
    row = lax.all_gather(own, "dp", axis=0, axis_index_groups=Z_GROUPS)
    kept, sent = project_low_rank(
        place, hidden, adapter_down_weight, layer_output_gradient, adapter_up_weight
    )
    last, kept, sent = together(last, kept, sent)
    b1, b2, b3 = move_y(last, 1), move_y(last, 2), move_y(last, -1)
    near = [layer_output_gradient, turn_x(layer_output_gradient)]
    kept = kept + swap_core(sent)
    kept = kept + swap_x(kept, lambda x: x ^ 1)
    chosen, weights = copied(chosen_expert_index, gates)
    kept, chosen, weights = together(kept, chosen, weights)
    kept = kept + swap_x(kept, lambda x: 3 - x)
    b1, b2, b3, kept, near[1] = together(b1, b2, b3, kept, near[1])
    column = jnp.stack([last, b1, b2, b3])
    b_blocks = lax.all_gather(column, "dp", axis=0, axis_index_groups=Z_GROUPS)

    other = swap_core(kept)
    *chunks, routed, gate_gradient = route(
        place, kept, other, chosen, weights, hidden, layer_output_gradient
    )
    near.append(turn_x(near[-1]))

    came = [move_y(chunks[j], j) for j in range(1, NY)]
    parts = sum(chunk.astype(jnp.float32) for chunk in [chunks[0]] + came)
    half = NZ // 2
    row, parts, near[2] = together(row, parts, near[2])
    halves = row[:half], row[half:]
    plus, minus = [move_y(piece, 1) for piece in halves], [move_y(piece, -1) for piece in halves]
    parts = lax.all_to_all(parts, "dp", 0, 0, tiled=True, axis_index_groups=Z_GROUPS)
    total = jnp.sum(parts, axis=0) * token_scale
    near.append(turn_x(near[-1]))
    plus[0], minus[1], total, near[3] = together(plus[0], minus[1], total, near[3])

    low, high = move_y(plus[0], 1), move_y(minus[1], -1)
    down_rows = hidden.shape[1] // n
    down = jnp.broadcast_to(total[:down_rows].astype(jnp.bfloat16)[None], (NZ, down_rows, 128))
    down = lax.all_to_all(down, "dp", 0, 0, tiled=True, axis_index_groups=Z_GROUPS)
    left = arrange(place, near + [swap_core(block) for block in near])
    plus[1], minus[0], down, total, left = together(plus[1], minus[0], down, total, left)

    partial, late_left = project_early(place, left, routed, adapter_down_weight, row, *plus, *minus)
    came = [down] + [move_y(down, j) for j in range(1, NY)]
    pairs = [(d * 8 + t, (4 * t + d // 8) * 8 + d % 8) for d in range(n) for t in range(8)]
    up_factor_gradient = lax.ppermute(total[down_rows:], ("dp", "tensor"), pairs).T
    hidden_input_gradient = project_last_rows(place, left, routed, adapter_down_weight, b_blocks)
    hidden_input_gradient, low, high, partial, up_factor_gradient, *came = together(
        hidden_input_gradient, low, high, partial, up_factor_gradient, *came
    )
    hidden_input_gradient = project_late(late_left, partial, low, high, hidden_input_gradient)
    came = jnp.stack([came[(3 - i) % NY] for i in range(2 * NY - 1)])
    came = lax.dynamic_slice_in_dim(came, 3 - place[1], NY, axis=0)
    down_factor_gradient = came.transpose(1, 0, 2, 3).reshape(-1, 128).astype(jnp.float32)
    return (hidden_input_gradient, down_factor_gradient, up_factor_gradient, gate_gradient)


def solution(mesh):
    return jax.shard_map(
        per_device,
        mesh=mesh,
        in_specs=(
            P("dp", "tensor"),
            P("dp", "tensor"),
            P("tensor", "dp"),
            P("tensor", None),
            P(),
            P("dp", None),
            P("dp", None),
        ),
        out_specs=(P("dp", "tensor"), P("tensor", None), P(None, ("dp", "tensor")), P("dp", None)),
        check_vma=False,
    )
```

```python
import jax
import jax.numpy as jnp
from jax import lax
from jax.experimental import pallas as pl
from jax.experimental.pallas import tpu as pltpu
from jax.sharding import PartitionSpec as P

EXPERTS = 8
RANK = 16
SCALE = 2.0
NZ, NY, NX = 8, 4, 4
ROWS_A = 1024
TILE = 256
Z_GROUPS = [[z * NY + y for z in range(NZ)] for y in range(NY)]
VMEM_BYTES = 60 * 1024 * 1024
LAST = (((1,), (1,)), ((), ()))
FIRST = (((0,), (0,)), ((), ()))


def move_y(value, step):
    pairs = [(z * NY + y, z * NY + (y + step) % NY) for z in range(NZ) for y in range(NY)]
    return lax.ppermute(value, "dp", pairs)


def turn_x(value):
    pairs = [(x * 2 + c, (x + 1 - 2 * c) % NX * 2 + c) for x in range(NX) for c in range(2)]
    return lax.ppermute(value, "tensor", pairs)


def swap_x(value, partner):
    return lax.ppermute(value, "tensor", [(x * 2 + c, partner(x) * 2 + c) for x in range(NX) for c in range(2)])


def swap_core(value):
    return lax.ppermute(value, "tensor", [(i, i ^ 1) for i in range(2 * NX)])


def full(*shape):
    return pl.BlockSpec(shape, lambda n: (0,) * len(shape))


def smem():
    return pl.BlockSpec(memory_space=pltpu.SMEM)


PARAMS = pltpu.CompilerParams(vmem_limit_bytes=VMEM_BYTES)
LIGHT = pl.CostEstimate(flops=0, bytes_accessed=0, transcendentals=0)


def project_low_rank_kernel(place, hidden, factor, gradient, up, kept, sent):
    half = kept.shape[0]
    width = gradient.shape[1]
    tensor = place[2] * 2 + place[3]
    lanes = pl.ds(pl.multiple_of(tensor * width, width), width)
    mine = pl.ds(pl.multiple_of(place[3] * half, half), half)
    other = pl.ds(pl.multiple_of((1 - place[3]) * half, half), half)
    for rows, out in ((mine, kept), (other, sent)):
        out[:, :128] = jnp.dot(hidden[rows, :], factor[...], preferred_element_type=jnp.float32)
        out[:, 128:] = lax.dot_general(
            gradient[rows, :], up[:, lanes], LAST, preferred_element_type=jnp.float32
        )


def project_low_rank(place, hidden, factor, gradient, up):
    half = jax.ShapeDtypeStruct((hidden.shape[0] // 2, 256), jnp.float32)
    return pl.pallas_call(
        project_low_rank_kernel,
        grid=(1,),
        out_shape=(half, half),
        in_specs=[smem()] + [full(*value.shape) for value in (hidden, factor, gradient, up)],
        out_specs=(full(*half.shape), full(*half.shape)),
        compiler_params=PARAMS,
        cost_estimate=LIGHT,
    )(place, hidden, factor, gradient, up)


def route_kernel(place, kept, other, chosen, gates, hidden, gradient, *refs):
    chunks, (routed, gate_gradient, parts) = refs[:NY], refs[NY:]
    zero = place[3] == 0
    both = jnp.concatenate(
        [jnp.where(zero, kept[...], other[...]), jnp.where(zero, other[...], kept[...])], axis=0
    )
    inner, outer = both[:, :128], both[:, 128:]
    expert = lax.broadcasted_iota(jnp.int32, inner.shape, 1) // RANK
    hits = [chosen[:, k : k + 1] == expert for k in range(2)]
    weight = jnp.where(hits[0], gates[:, 0:1], 0.0) + jnp.where(hits[1], gates[:, 1:2], 0.0)
    routed_outer = (SCALE * weight * outer).astype(jnp.bfloat16)
    routed_inner = (SCALE * weight * inner).astype(jnp.bfloat16)
    routed[...] = routed_outer
    product = inner * outer
    for k in range(2):
        picked = jnp.where(hits[k], product, 0.0)
        gate_gradient[:, k : k + 1] = SCALE * jnp.sum(picked, axis=1, keepdims=True)
    down = lax.dot_general(hidden[...], routed_outer, FIRST, preferred_element_type=jnp.float32)
    up = lax.dot_general(gradient[...], routed_inner, FIRST, preferred_element_type=jnp.float32)
    n = NZ * NY
    for whole_sum, first in ((down, 0), (up, down.shape[0] // n)):
        rows = whole_sum.shape[0] // n
        pieces = whole_sum.astype(jnp.bfloat16).reshape(NZ, NY, rows, 128)
        for y in range(NY):
            parts[y, :, pl.ds(first, rows), :] = pieces[:, y]
    for j, chunk in enumerate(chunks):
        chunk[...] = parts[lax.rem(place[1] + j, NY)]


def route(place, kept, other, chosen, gates, hidden, gradient):
    n = NZ * NY
    tokens = hidden.shape[0]
    rows = (hidden.shape[1] + gradient.shape[1]) // n
    outs = (
        *[jax.ShapeDtypeStruct((NZ, rows, 128), jnp.bfloat16)] * NY,
        jax.ShapeDtypeStruct((tokens, 128), jnp.bfloat16),
        jax.ShapeDtypeStruct((tokens, 2), jnp.float32),
    )
    return pl.pallas_call(
        route_kernel,
        grid=(1,),
        out_shape=outs,
        in_specs=[smem()]
        + [full(*value.shape) for value in (kept, other, chosen, gates, hidden, gradient)],
        out_specs=tuple(full(*out.shape) for out in outs),
        scratch_shapes=[pltpu.VMEM((NY, NZ, rows, 128), jnp.bfloat16)],
        compiler_params=PARAMS,
        cost_estimate=LIGHT,
    )(place, kept, other, chosen, gates, hidden, gradient)


def copied(*values):
    def kernel(*refs):
        for i in range(len(values)):
            refs[len(values) + i][...] = refs[i][...]

    specs = [full(*value.shape) for value in values]
    return pl.pallas_call(
        kernel,
        grid=(1,),
        out_shape=tuple(jax.ShapeDtypeStruct(value.shape, value.dtype) for value in values),
        in_specs=specs,
        out_specs=tuple(specs),
        compiler_params=PARAMS,
        cost_estimate=LIGHT,
    )(*values)


def arrange_kernel(place, *refs):
    out = refs[-1]
    x, c = place[2], place[3]
    sign = 1 - 2 * c
    width = out.shape[1] // 8
    for step in range(NX):
        for block, turn, core in ((refs[step], sign, c), (refs[NX + step], -sign, 1 - c)):
            owner = lax.rem(x - turn * step + 2 * NX, NX) * 2 + core
            out[:, pl.ds(pl.multiple_of(owner * width, width), width)] = block[...]


def arrange(place, blocks):
    tokens, width = blocks[0].shape
    return pl.pallas_call(
        arrange_kernel,
        grid=(1,),
        out_shape=jax.ShapeDtypeStruct((tokens, width * 8), jnp.bfloat16),
        in_specs=[smem()] + [full(*block.shape) for block in blocks],
        out_specs=full(tokens, width * 8),
        compiler_params=PARAMS,
        cost_estimate=LIGHT,
    )(place, *blocks)


A_TILES = ROWS_A // TILE


A_TILES = ROWS_A // TILE


def lanes_of(place, z, dy):
    owner = z * NY + lax.rem(place[1] - dy + NY, NY)
    return pl.ds(pl.multiple_of(owner * 128, 128), 128)


def own_kernel(place, left, routed, factor, own, out, sides, later, picked):
    @pl.when(pl.program_id(0) == 0)
    def _():
        for z in range(NZ):
            lanes = pl.ds(z * 128, 128)
            picked[:, lanes] = left[:, lanes_of(place, z, 0)]
            sides[:, lanes] = left[:, lanes_of(place, z, 1)]
            sides[:, pl.ds((NZ + z) * 128, 128)] = left[:, lanes_of(place, z, -1)]
            later[:, lanes] = left[:, lanes_of(place, z, 2)]

    right = jnp.concatenate([own[z] for z in range(NZ)], axis=1)
    total = lax.dot_general(picked[...], right, LAST, preferred_element_type=jnp.float32)
    total += lax.dot_general(routed[...], factor[...], LAST, preferred_element_type=jnp.float32)
    out[...] = total


def sides_kernel(picked, partial, plus, minus, out):
    right = jnp.concatenate([side[z] for side in (plus, minus) for z in range(NZ)], axis=1)
    total = lax.dot_general(picked[...], right, LAST, preferred_element_type=jnp.float32)
    out[...] = total + partial[...]


def last_rows_kernel(place, left, routed, factor, blocks, out, right):
    for z in range(NZ):
        for dy in range(NY):
            right[:, lanes_of(place, z, dy)] = blocks[z, dy]
    total = lax.dot_general(left[...], right[...], LAST, preferred_element_type=jnp.float32)
    total += lax.dot_general(routed[...], factor[...], LAST, preferred_element_type=jnp.float32)
    out[...] = total.astype(out.dtype)


def late_kernel(picked, partial, low, high, base, out):
    del base
    blocks = [low[z] for z in range(NZ // 2)] + [high[z] for z in range(NZ // 2)]
    right = jnp.concatenate(blocks, axis=1)
    total = lax.dot_general(picked[...], right, LAST, preferred_element_type=jnp.float32)
    out[...] = (total + partial[...]).astype(out.dtype)


def whole(shape):
    return pl.BlockSpec(shape, lambda n: (0,) * len(shape), pipeline_mode=pl.Buffered(1))


def project_own(place, left, routed, factor, own):
    tokens, depth = left.shape
    used = depth // NY
    return pl.pallas_call(
        own_kernel,
        grid=(A_TILES,),
        out_shape=(
            jax.ShapeDtypeStruct((tokens, ROWS_A), jnp.float32),
            jax.ShapeDtypeStruct((tokens, 2 * used), jnp.bfloat16),
            jax.ShapeDtypeStruct((tokens, used), jnp.bfloat16),
        ),
        in_specs=[smem(), whole((tokens, depth)), whole((tokens, 128))]
        + [pl.BlockSpec((TILE, 128), lambda n: (n, 0))]
        + [pl.BlockSpec((NZ, TILE, 128), lambda n: (0, n, 0))],
        out_specs=(
            pl.BlockSpec((tokens, TILE), lambda n: (0, n)),
            pl.BlockSpec((tokens, 2 * used), lambda n: (0, 0)),
            pl.BlockSpec((tokens, used), lambda n: (0, 0)),
        ),
        scratch_shapes=[pltpu.VMEM((tokens, used), jnp.bfloat16)],
        compiler_params=PARAMS,
        cost_estimate=LIGHT,
    )(place, left, routed, factor, own)


def project_sides(picked, partial, plus, minus):
    tokens, depth = picked.shape
    return pl.pallas_call(
        sides_kernel,
        grid=(A_TILES,),
        out_shape=jax.ShapeDtypeStruct(partial.shape, jnp.float32),
        in_specs=[whole((tokens, depth)), pl.BlockSpec((tokens, TILE), lambda n: (0, n))]
        + [pl.BlockSpec((NZ, TILE, 128), lambda n: (0, n, 0))] * 2,
        out_specs=pl.BlockSpec((tokens, TILE), lambda n: (0, n)),
        compiler_params=PARAMS,
        cost_estimate=LIGHT,
    )(picked, partial, plus, minus)


def project_last_rows(place, left, routed, factor, blocks):
    tokens, depth = left.shape
    units = factor.shape[0]
    return pl.pallas_call(
        last_rows_kernel,
        grid=(units // TILE - A_TILES,),
        out_shape=jax.ShapeDtypeStruct((tokens, units), jnp.bfloat16),
        in_specs=[smem(), whole((tokens, depth)), whole((tokens, 128))]
        + [
            pl.BlockSpec((TILE, 128), lambda n: (n + A_TILES, 0)),
            pl.BlockSpec((NZ, NY, TILE, 128), lambda n: (0, 0, n, 0)),
        ],
        out_specs=pl.BlockSpec((tokens, TILE), lambda n: (0, n + A_TILES)),
        scratch_shapes=[pltpu.VMEM((TILE, depth), jnp.bfloat16)],
        compiler_params=PARAMS,
        cost_estimate=LIGHT,
    )(place, left, routed, factor, blocks)


def project_late(picked, partial, low, high, base):
    tokens, depth = picked.shape
    return pl.pallas_call(
        late_kernel,
        grid=(A_TILES,),
        out_shape=jax.ShapeDtypeStruct(base.shape, jnp.bfloat16),
        in_specs=[whole((tokens, depth)), pl.BlockSpec((tokens, TILE), lambda n: (0, n))]
        + [pl.BlockSpec((NZ // 2, TILE, 128), lambda n: (0, n, 0))] * 2
        + [pl.BlockSpec(memory_space=pl.ANY)],
        out_specs=pl.BlockSpec((tokens, TILE), lambda n: (0, n)),
        input_output_aliases={4: 0},
        compiler_params=PARAMS,
        cost_estimate=LIGHT,
    )(picked, partial, low, high, base)


def per_device(
    hidden,
    layer_output_gradient,
    frozen_down_weight,
    adapter_down_weight,
    adapter_up_weight,
    chosen_expert_index,
    gates,
):
    together = lambda *values: lax.optimization_barrier(values)
    dp_index = lax.axis_index("dp").astype(jnp.int32)
    tensor_index = lax.axis_index("tensor").astype(jnp.int32)
    place = jnp.stack(
        [lax.div(dp_index, NY), lax.rem(dp_index, NY), lax.div(tensor_index, 2), lax.rem(tensor_index, 2)]
    )
    tokens_here = hidden.shape[0]
    token_scale = float(tokens_here * NZ * NY) ** (-0.5)
    n = NZ * NY

    own, last = frozen_down_weight[:ROWS_A], frozen_down_weight[ROWS_A:]
    row = lax.all_gather(own, "dp", axis=0, axis_index_groups=Z_GROUPS)
    kept, sent = project_low_rank(
        place, hidden, adapter_down_weight, layer_output_gradient, adapter_up_weight
    )
    last, kept, sent = together(last, kept, sent)
    b1, b2, b3 = move_y(last, 1), move_y(last, 2), move_y(last, -1)
    near = [layer_output_gradient, turn_x(layer_output_gradient)]
    kept = kept + swap_core(sent)
    kept = kept + swap_x(kept, lambda x: x ^ 1)
    chosen, weights = copied(chosen_expert_index, gates)
    kept, chosen, weights = together(kept, chosen, weights)
    kept = kept + swap_x(kept, lambda x: 3 - x)
    b1, b2, b3, kept, near[1] = together(b1, b2, b3, kept, near[1])
    column = jnp.stack([last, b1, b2, b3])
    b_blocks = lax.all_gather(column, "dp", axis=0, axis_index_groups=Z_GROUPS)

    other = swap_core(kept)
    *chunks, routed, gate_gradient = route(
        place, kept, other, chosen, weights, hidden, layer_output_gradient
    )
    near.append(turn_x(near[-1]))

    came = [move_y(chunks[j], j) for j in range(1, NY)]
    parts = sum(chunk.astype(jnp.float32) for chunk in [chunks[0]] + came)
    row, parts, near[2] = together(row, parts, near[2])
    plus, minus = move_y(row, 1), move_y(row, -1)
    parts = lax.all_to_all(parts, "dp", 0, 0, tiled=True, axis_index_groups=Z_GROUPS)
    total = jnp.sum(parts, axis=0) * token_scale
    down_rows = hidden.shape[1] // n
    down = jnp.broadcast_to(total[:down_rows].astype(jnp.bfloat16)[None], (NZ, down_rows, 128))
    down = lax.all_to_all(down, "dp", 0, 0, tiled=True, axis_index_groups=Z_GROUPS)
    near.append(turn_x(near[-1]))
    left = arrange(place, near + [swap_core(block) for block in near])
    partial, side_left, late_left = project_own(place, left, routed, adapter_down_weight, row)
    down, partial, side_left, late_left = together(down, partial, side_left, late_left)
    came = [down] + [move_y(down, j) for j in range(1, NY)]
    plus, minus, partial, side_left, late_left, *came = together(
        plus, minus, partial, side_left, late_left, *came
    )

    half = NZ // 2
    low, high = move_y(plus[:half], 1), move_y(minus[half:], -1)
    partial = project_sides(side_left, partial, plus, minus)
    pairs = [(d * 8 + t, (4 * t + d // 8) * 8 + d % 8) for d in range(n) for t in range(8)]
    up_factor_gradient = lax.ppermute(total[down_rows:], ("dp", "tensor"), pairs).T
    came = jnp.stack([came[(3 - i) % NY] for i in range(2 * NY - 1)])
    came = lax.dynamic_slice_in_dim(came, 3 - place[1], NY, axis=0)
    down_factor_gradient = came.transpose(1, 0, 2, 3).reshape(-1, 128).astype(jnp.float32)

    hidden_input_gradient = project_last_rows(place, left, routed, adapter_down_weight, b_blocks)
    hidden_input_gradient, low, high, partial, down_factor_gradient, up_factor_gradient = together(
        hidden_input_gradient, low, high, partial, down_factor_gradient, up_factor_gradient
    )
    hidden_input_gradient = project_late(late_left, partial, low, high, hidden_input_gradient)
    return (hidden_input_gradient, down_factor_gradient, up_factor_gradient, gate_gradient)


def solution(mesh):
    return jax.shard_map(
        per_device,
        mesh=mesh,
        in_specs=(
            P("dp", "tensor"),
            P("dp", "tensor"),
            P("tensor", "dp"),
            P("tensor", None),
            P(),
            P("dp", None),
            P("dp", None),
        ),
        out_specs=(P("dp", "tensor"), P("tensor", None), P(None, ("dp", "tensor")), P("dp", None)),
        check_vma=False,
    )
```

```python
import jax
import jax.numpy as jnp
from jax import lax
from jax.experimental import pallas as pl
from jax.experimental.pallas import tpu as pltpu
from jax.sharding import PartitionSpec as P

EXPERTS = 8
RANK = 16
SCALE = 2.0
NZ, NY, NX = 8, 4, 4
ROWS_A = 1024
TILE = 256
Z_GROUPS = [[z * NY + y for z in range(NZ)] for y in range(NY)]
VMEM_BYTES = 60 * 1024 * 1024
LAST = (((1,), (1,)), ((), ()))
FIRST = (((0,), (0,)), ((), ()))


def move_y(value, step):
    pairs = [(z * NY + y, z * NY + (y + step) % NY) for z in range(NZ) for y in range(NY)]
    return lax.ppermute(value, "dp", pairs)


def turn_x(value):
    pairs = [(x * 2 + c, (x + 1 - 2 * c) % NX * 2 + c) for x in range(NX) for c in range(2)]
    return lax.ppermute(value, "tensor", pairs)


def swap_x(value, partner):
    return lax.ppermute(value, "tensor", [(x * 2 + c, partner(x) * 2 + c) for x in range(NX) for c in range(2)])


def swap_core(value):
    return lax.ppermute(value, "tensor", [(i, i ^ 1) for i in range(2 * NX)])


def full(*shape):
    return pl.BlockSpec(shape, lambda n: (0,) * len(shape))


def smem():
    return pl.BlockSpec(memory_space=pltpu.SMEM)


PARAMS = pltpu.CompilerParams(vmem_limit_bytes=VMEM_BYTES)
LIGHT = pl.CostEstimate(flops=0, bytes_accessed=0, transcendentals=0)


def project_low_rank_kernel(place, hidden, factor, gradient, up, kept, sent):
    half = kept.shape[0]
    width = gradient.shape[1]
    tensor = place[2] * 2 + place[3]
    lanes = pl.ds(pl.multiple_of(tensor * width, width), width)
    mine = pl.ds(pl.multiple_of(place[3] * half, half), half)
    other = pl.ds(pl.multiple_of((1 - place[3]) * half, half), half)
    for rows, out in ((mine, kept), (other, sent)):
        out[:, :128] = jnp.dot(hidden[rows, :], factor[...], preferred_element_type=jnp.float32)
        out[:, 128:] = lax.dot_general(
            gradient[rows, :], up[:, lanes], LAST, preferred_element_type=jnp.float32
        )


def project_low_rank(place, hidden, factor, gradient, up):
    half = jax.ShapeDtypeStruct((hidden.shape[0] // 2, 256), jnp.float32)
    return pl.pallas_call(
        project_low_rank_kernel,
        grid=(1,),
        out_shape=(half, half),
        in_specs=[smem()] + [full(*value.shape) for value in (hidden, factor, gradient, up)],
        out_specs=(full(*half.shape), full(*half.shape)),
        compiler_params=PARAMS,
        cost_estimate=LIGHT,
    )(place, hidden, factor, gradient, up)


def route_kernel(place, kept, other, chosen, gates, hidden, gradient, *refs):
    chunks, (routed, gate_gradient, parts) = refs[:NY], refs[NY:]
    zero = place[3] == 0
    both = jnp.concatenate(
        [jnp.where(zero, kept[...], other[...]), jnp.where(zero, other[...], kept[...])], axis=0
    )
    inner, outer = both[:, :128], both[:, 128:]
    expert = lax.broadcasted_iota(jnp.int32, inner.shape, 1) // RANK
    hits = [chosen[:, k : k + 1] == expert for k in range(2)]
    weight = jnp.where(hits[0], gates[:, 0:1], 0.0) + jnp.where(hits[1], gates[:, 1:2], 0.0)
    routed_outer = (SCALE * weight * outer).astype(jnp.bfloat16)
    routed_inner = (SCALE * weight * inner).astype(jnp.bfloat16)
    routed[...] = routed_outer
    product = inner * outer
    for k in range(2):
        picked = jnp.where(hits[k], product, 0.0)
        gate_gradient[:, k : k + 1] = SCALE * jnp.sum(picked, axis=1, keepdims=True)
    down = lax.dot_general(hidden[...], routed_outer, FIRST, preferred_element_type=jnp.float32)
    up = lax.dot_general(gradient[...], routed_inner, FIRST, preferred_element_type=jnp.float32)
    n = NZ * NY
    for whole_sum, first in ((down, 0), (up, down.shape[0] // n)):
        rows = whole_sum.shape[0] // n
        pieces = whole_sum.astype(jnp.bfloat16).reshape(NZ, NY, rows, 128)
        for y in range(NY):
            parts[y, :, pl.ds(first, rows), :] = pieces[:, y]
    for j, chunk in enumerate(chunks):
        chunk[...] = parts[lax.rem(place[1] + j, NY)]


def route(place, kept, other, chosen, gates, hidden, gradient):
    n = NZ * NY
    tokens = hidden.shape[0]
    rows = (hidden.shape[1] + gradient.shape[1]) // n
    outs = (
        *[jax.ShapeDtypeStruct((NZ, rows, 128), jnp.bfloat16)] * NY,
        jax.ShapeDtypeStruct((tokens, 128), jnp.bfloat16),
        jax.ShapeDtypeStruct((tokens, 2), jnp.float32),
    )
    return pl.pallas_call(
        route_kernel,
        grid=(1,),
        out_shape=outs,
        in_specs=[smem()]
        + [full(*value.shape) for value in (kept, other, chosen, gates, hidden, gradient)],
        out_specs=tuple(full(*out.shape) for out in outs),
        scratch_shapes=[pltpu.VMEM((NY, NZ, rows, 128), jnp.bfloat16)],
        compiler_params=PARAMS,
        cost_estimate=LIGHT,
    )(place, kept, other, chosen, gates, hidden, gradient)


def copied(*values):
    def kernel(*refs):
        for i in range(len(values)):
            refs[len(values) + i][...] = refs[i][...]

    specs = [full(*value.shape) for value in values]
    return pl.pallas_call(
        kernel,
        grid=(1,),
        out_shape=tuple(jax.ShapeDtypeStruct(value.shape, value.dtype) for value in values),
        in_specs=specs,
        out_specs=tuple(specs),
        compiler_params=PARAMS,
        cost_estimate=LIGHT,
    )(*values)


def arrange_kernel(place, *refs):
    out = refs[-1]
    x, c = place[2], place[3]
    sign = 1 - 2 * c
    width = out.shape[1] // 8
    for step in range(NX):
        for block, turn, core in ((refs[step], sign, c), (refs[NX + step], -sign, 1 - c)):
            owner = lax.rem(x - turn * step + 2 * NX, NX) * 2 + core
            out[:, pl.ds(pl.multiple_of(owner * width, width), width)] = block[...]


def arrange(place, blocks):
    tokens, width = blocks[0].shape
    return pl.pallas_call(
        arrange_kernel,
        grid=(1,),
        out_shape=jax.ShapeDtypeStruct((tokens, width * 8), jnp.bfloat16),
        in_specs=[smem()] + [full(*block.shape) for block in blocks],
        out_specs=full(tokens, width * 8),
        compiler_params=PARAMS,
        cost_estimate=LIGHT,
    )(place, *blocks)


A_TILES = ROWS_A // TILE


A_TILES = ROWS_A // TILE


def lanes_of(place, z, dy):
    owner = z * NY + lax.rem(place[1] - dy + NY, NY)
    return pl.ds(pl.multiple_of(owner * 128, 128), 128)


def own_kernel(place, left, routed, factor, own, out, sides, later, picked):
    @pl.when(pl.program_id(0) == 0)
    def _():
        for z in range(NZ):
            lanes = pl.ds(z * 128, 128)
            picked[:, lanes] = left[:, lanes_of(place, z, 0)]
            sides[:, lanes] = left[:, lanes_of(place, z, 1)]
            sides[:, pl.ds((NZ + z) * 128, 128)] = left[:, lanes_of(place, z, -1)]
            later[:, lanes] = left[:, lanes_of(place, z, 2)]

    right = jnp.concatenate([own[z] for z in range(NZ)], axis=1)
    total = lax.dot_general(picked[...], right, LAST, preferred_element_type=jnp.float32)
    total += lax.dot_general(routed[...], factor[...], LAST, preferred_element_type=jnp.float32)
    out[...] = total


def sides_kernel(picked, partial, plus, minus, out):
    right = jnp.concatenate([side[z] for side in (plus, minus) for z in range(NZ)], axis=1)
    total = lax.dot_general(picked[...], right, LAST, preferred_element_type=jnp.float32)
    out[...] = total + partial[...]


def last_rows_kernel(place, left, routed, factor, blocks, out, right):
    for z in range(NZ):
        for dy in range(NY):
            right[:, lanes_of(place, z, dy)] = blocks[z, dy]
    total = lax.dot_general(left[...], right[...], LAST, preferred_element_type=jnp.float32)
    total += lax.dot_general(routed[...], factor[...], LAST, preferred_element_type=jnp.float32)
    out[...] = total.astype(out.dtype)


def late_kernel(picked, partial, low, high, base, out):
    del base
    blocks = [low[z] for z in range(NZ // 2)] + [high[z] for z in range(NZ // 2)]
    right = jnp.concatenate(blocks, axis=1)
    total = lax.dot_general(picked[...], right, LAST, preferred_element_type=jnp.float32)
    out[...] = (total + partial[...]).astype(out.dtype)


def whole(shape):
    return pl.BlockSpec(shape, lambda n: (0,) * len(shape), pipeline_mode=pl.Buffered(1))


def project_own(place, left, routed, factor, own):
    tokens, depth = left.shape
    used = depth // NY
    return pl.pallas_call(
        own_kernel,
        grid=(A_TILES,),
        out_shape=(
            jax.ShapeDtypeStruct((tokens, ROWS_A), jnp.float32),
            jax.ShapeDtypeStruct((tokens, 2 * used), jnp.bfloat16),
            jax.ShapeDtypeStruct((tokens, used), jnp.bfloat16),
        ),
        in_specs=[smem(), whole((tokens, depth)), whole((tokens, 128))]
        + [pl.BlockSpec((TILE, 128), lambda n: (n, 0))]
        + [pl.BlockSpec((NZ, TILE, 128), lambda n: (0, n, 0))],
        out_specs=(
            pl.BlockSpec((tokens, TILE), lambda n: (0, n)),
            pl.BlockSpec((tokens, 2 * used), lambda n: (0, 0)),
            pl.BlockSpec((tokens, used), lambda n: (0, 0)),
        ),
        scratch_shapes=[pltpu.VMEM((tokens, used), jnp.bfloat16)],
        compiler_params=PARAMS,
        cost_estimate=LIGHT,
    )(place, left, routed, factor, own)


def project_sides(picked, partial, plus, minus):
    tokens, depth = picked.shape
    return pl.pallas_call(
        sides_kernel,
        grid=(A_TILES,),
        out_shape=jax.ShapeDtypeStruct(partial.shape, jnp.float32),
        in_specs=[whole((tokens, depth)), pl.BlockSpec((tokens, TILE), lambda n: (0, n))]
        + [pl.BlockSpec((NZ, TILE, 128), lambda n: (0, n, 0))] * 2,
        out_specs=pl.BlockSpec((tokens, TILE), lambda n: (0, n)),
        compiler_params=PARAMS,
        cost_estimate=LIGHT,
    )(picked, partial, plus, minus)


def project_last_rows(place, left, routed, factor, blocks):
    tokens, depth = left.shape
    units = factor.shape[0]
    return pl.pallas_call(
        last_rows_kernel,
        grid=(units // TILE - A_TILES,),
        out_shape=jax.ShapeDtypeStruct((tokens, units), jnp.bfloat16),
        in_specs=[smem(), whole((tokens, depth)), whole((tokens, 128))]
        + [
            pl.BlockSpec((TILE, 128), lambda n: (n + A_TILES, 0)),
            pl.BlockSpec((NZ, NY, TILE, 128), lambda n: (0, 0, n, 0)),
        ],
        out_specs=pl.BlockSpec((tokens, TILE), lambda n: (0, n + A_TILES)),
        scratch_shapes=[pltpu.VMEM((TILE, depth), jnp.bfloat16)],
        compiler_params=PARAMS,
        cost_estimate=LIGHT,
    )(place, left, routed, factor, blocks)


def project_late(picked, partial, low, high, base):
    tokens, depth = picked.shape
    return pl.pallas_call(
        late_kernel,
        grid=(A_TILES,),
        out_shape=jax.ShapeDtypeStruct(base.shape, jnp.bfloat16),
        in_specs=[whole((tokens, depth)), pl.BlockSpec((tokens, TILE), lambda n: (0, n))]
        + [pl.BlockSpec((NZ // 2, TILE, 128), lambda n: (0, n, 0))] * 2
        + [pl.BlockSpec(memory_space=pl.ANY)],
        out_specs=pl.BlockSpec((tokens, TILE), lambda n: (0, n)),
        input_output_aliases={4: 0},
        compiler_params=PARAMS,
        cost_estimate=LIGHT,
    )(picked, partial, low, high, base)


def per_device(
    hidden,
    layer_output_gradient,
    frozen_down_weight,
    adapter_down_weight,
    adapter_up_weight,
    chosen_expert_index,
    gates,
):
    together = lambda *values: lax.optimization_barrier(values)
    dp_index = lax.axis_index("dp").astype(jnp.int32)
    tensor_index = lax.axis_index("tensor").astype(jnp.int32)
    place = jnp.stack(
        [lax.div(dp_index, NY), lax.rem(dp_index, NY), lax.div(tensor_index, 2), lax.rem(tensor_index, 2)]
    )
    tokens_here = hidden.shape[0]
    token_scale = float(tokens_here * NZ * NY) ** (-0.5)
    n = NZ * NY

    own, last = frozen_down_weight[:ROWS_A], frozen_down_weight[ROWS_A:]
    row = lax.all_gather(own, "dp", axis=0, axis_index_groups=Z_GROUPS)
    kept, sent = project_low_rank(
        place, hidden, adapter_down_weight, layer_output_gradient, adapter_up_weight
    )
    last, kept, sent = together(last, kept, sent)
    b1, b2, b3 = move_y(last, 1), move_y(last, 2), move_y(last, -1)
    near = [layer_output_gradient, turn_x(layer_output_gradient)]
    kept = kept + swap_core(sent)
    kept = kept + swap_x(kept, lambda x: x ^ 1)
    chosen, weights = copied(chosen_expert_index, gates)
    kept, chosen, weights = together(kept, chosen, weights)
    kept = kept + swap_x(kept, lambda x: 3 - x)
    b1, b2, b3, kept, near[1] = together(b1, b2, b3, kept, near[1])
    column = jnp.stack([last, b1, b2, b3])
    b_blocks = lax.all_gather(column, "dp", axis=0, axis_index_groups=Z_GROUPS)

    other = swap_core(kept)
    *chunks, routed, gate_gradient = route(
        place, kept, other, chosen, weights, hidden, layer_output_gradient
    )
    near.append(turn_x(near[-1]))

    came = [move_y(chunks[j], j) for j in range(1, NY)]
    parts = sum(chunk.astype(jnp.float32) for chunk in [chunks[0]] + came)
    row, parts, near[2] = together(row, parts, near[2])
    plus, minus = move_y(row, 1), move_y(row, -1)
    parts = lax.all_to_all(parts, "dp", 0, 0, tiled=True, axis_index_groups=Z_GROUPS)
    total = jnp.sum(parts, axis=0) * token_scale
    down_rows = hidden.shape[1] // n
    down = jnp.broadcast_to(total[:down_rows].astype(jnp.bfloat16)[None], (NZ, down_rows, 128))
    down = lax.all_to_all(down, "dp", 0, 0, tiled=True, axis_index_groups=Z_GROUPS)
    near.append(turn_x(near[-1]))
    left = arrange(place, near + [swap_core(block) for block in near])
    partial, side_left, late_left = project_own(place, left, routed, adapter_down_weight, row)
    plus, minus, partial, side_left, late_left, down, total = together(
        plus, minus, partial, side_left, late_left, down, total
    )

    half = NZ // 2
    low, high = move_y(plus[:half], 1), move_y(minus[half:], -1)
    partial = project_sides(side_left, partial, plus, minus)
    partial, down, total = together(partial, down, total)
    came = [down] + [move_y(down, j) for j in range(1, NY)]
    hidden_input_gradient = project_last_rows(place, left, routed, adapter_down_weight, b_blocks)
    hidden_input_gradient, low, high, partial, total, *came = together(
        hidden_input_gradient, low, high, partial, total, *came
    )
    pairs = [(d * 8 + t, (4 * t + d // 8) * 8 + d % 8) for d in range(n) for t in range(8)]
    up_factor_gradient = lax.ppermute(total[down_rows:], ("dp", "tensor"), pairs).T
    hidden_input_gradient = project_late(late_left, partial, low, high, hidden_input_gradient)
    came = jnp.stack([came[(3 - i) % NY] for i in range(2 * NY - 1)])
    came = lax.dynamic_slice_in_dim(came, 3 - place[1], NY, axis=0)
    down_factor_gradient = came.transpose(1, 0, 2, 3).reshape(-1, 128).astype(jnp.float32)
    return (hidden_input_gradient, down_factor_gradient, up_factor_gradient, gate_gradient)


def solution(mesh):
    return jax.shard_map(
        per_device,
        mesh=mesh,
        in_specs=(
            P("dp", "tensor"),
            P("dp", "tensor"),
            P("tensor", "dp"),
            P("tensor", None),
            P(),
            P("dp", None),
            P("dp", None),
        ),
        out_specs=(P("dp", "tensor"), P("tensor", None), P(None, ("dp", "tensor")), P("dp", None)),
        check_vma=False,
    )
```

```python
import jax
import jax.numpy as jnp
from jax import lax
from jax.experimental import pallas as pl
from jax.experimental.pallas import tpu as pltpu
from jax.sharding import PartitionSpec as P

EXPERTS = 8
RANK = 16
SCALE = 2.0
NZ, NY, NX = 8, 4, 4
ROWS_A = 1024
TILE = 256
Z_GROUPS = [[z * NY + y for z in range(NZ)] for y in range(NY)]
VMEM_BYTES = 60 * 1024 * 1024
LAST = (((1,), (1,)), ((), ()))
FIRST = (((0,), (0,)), ((), ()))


def move_y(value, step):
    pairs = [(z * NY + y, z * NY + (y + step) % NY) for z in range(NZ) for y in range(NY)]
    return lax.ppermute(value, "dp", pairs)


def turn_x(value):
    pairs = [(x * 2 + c, (x + 1 - 2 * c) % NX * 2 + c) for x in range(NX) for c in range(2)]
    return lax.ppermute(value, "tensor", pairs)


def swap_x(value, partner):
    return lax.ppermute(value, "tensor", [(x * 2 + c, partner(x) * 2 + c) for x in range(NX) for c in range(2)])


def swap_core(value):
    return lax.ppermute(value, "tensor", [(i, i ^ 1) for i in range(2 * NX)])


def full(*shape):
    return pl.BlockSpec(shape, lambda n: (0,) * len(shape))


def smem():
    return pl.BlockSpec(memory_space=pltpu.SMEM)


PARAMS = pltpu.CompilerParams(vmem_limit_bytes=VMEM_BYTES)
LIGHT = pl.CostEstimate(flops=0, bytes_accessed=0, transcendentals=0)


def project_low_rank_kernel(place, hidden, factor, gradient, up, kept, sent):
    half = kept.shape[0]
    width = gradient.shape[1]
    tensor = place[2] * 2 + place[3]
    lanes = pl.ds(pl.multiple_of(tensor * width, width), width)
    mine = pl.ds(pl.multiple_of(place[3] * half, half), half)
    other = pl.ds(pl.multiple_of((1 - place[3]) * half, half), half)
    for rows, out in ((mine, kept), (other, sent)):
        out[:, :128] = jnp.dot(hidden[rows, :], factor[...], preferred_element_type=jnp.float32)
        out[:, 128:] = lax.dot_general(
            gradient[rows, :], up[:, lanes], LAST, preferred_element_type=jnp.float32
        )


def project_low_rank(place, hidden, factor, gradient, up):
    half = jax.ShapeDtypeStruct((hidden.shape[0] // 2, 256), jnp.float32)
    return pl.pallas_call(
        project_low_rank_kernel,
        grid=(1,),
        out_shape=(half, half),
        in_specs=[smem()] + [full(*value.shape) for value in (hidden, factor, gradient, up)],
        out_specs=(full(*half.shape), full(*half.shape)),
        compiler_params=PARAMS,
        cost_estimate=LIGHT,
    )(place, hidden, factor, gradient, up)


def route_kernel(place, kept, other, chosen, gates, hidden, gradient, *refs):
    chunks, (routed, gate_gradient, parts) = refs[:NY], refs[NY:]
    zero = place[3] == 0
    both = jnp.concatenate(
        [jnp.where(zero, kept[...], other[...]), jnp.where(zero, other[...], kept[...])], axis=0
    )
    inner, outer = both[:, :128], both[:, 128:]
    expert = lax.broadcasted_iota(jnp.int32, inner.shape, 1) // RANK
    hits = [chosen[:, k : k + 1] == expert for k in range(2)]
    weight = jnp.where(hits[0], gates[:, 0:1], 0.0) + jnp.where(hits[1], gates[:, 1:2], 0.0)
    routed_outer = (SCALE * weight * outer).astype(jnp.bfloat16)
    routed_inner = (SCALE * weight * inner).astype(jnp.bfloat16)
    routed[...] = routed_outer
    product = inner * outer
    for k in range(2):
        picked = jnp.where(hits[k], product, 0.0)
        gate_gradient[:, k : k + 1] = SCALE * jnp.sum(picked, axis=1, keepdims=True)
    down = lax.dot_general(hidden[...], routed_outer, FIRST, preferred_element_type=jnp.float32)
    up = lax.dot_general(gradient[...], routed_inner, FIRST, preferred_element_type=jnp.float32)
    n = NZ * NY
    for whole_sum, first in ((down, 0), (up, down.shape[0] // n)):
        rows = whole_sum.shape[0] // n
        pieces = whole_sum.astype(jnp.bfloat16).reshape(NZ, NY, rows, 128)
        for y in range(NY):
            parts[y, :, pl.ds(first, rows), :] = pieces[:, y]
    for j, chunk in enumerate(chunks):
        chunk[...] = parts[lax.rem(place[1] + j, NY)]


def route(place, kept, other, chosen, gates, hidden, gradient):
    n = NZ * NY
    tokens = hidden.shape[0]
    rows = (hidden.shape[1] + gradient.shape[1]) // n
    outs = (
        *[jax.ShapeDtypeStruct((NZ, rows, 128), jnp.bfloat16)] * NY,
        jax.ShapeDtypeStruct((tokens, 128), jnp.bfloat16),
        jax.ShapeDtypeStruct((tokens, 2), jnp.float32),
    )
    return pl.pallas_call(
        route_kernel,
        grid=(1,),
        out_shape=outs,
        in_specs=[smem()]
        + [full(*value.shape) for value in (kept, other, chosen, gates, hidden, gradient)],
        out_specs=tuple(full(*out.shape) for out in outs),
        scratch_shapes=[pltpu.VMEM((NY, NZ, rows, 128), jnp.bfloat16)],
        compiler_params=PARAMS,
        cost_estimate=LIGHT,
    )(place, kept, other, chosen, gates, hidden, gradient)


def copied(*values):
    def kernel(*refs):
        for i in range(len(values)):
            refs[len(values) + i][...] = refs[i][...]

    specs = [full(*value.shape) for value in values]
    return pl.pallas_call(
        kernel,
        grid=(1,),
        out_shape=tuple(jax.ShapeDtypeStruct(value.shape, value.dtype) for value in values),
        in_specs=specs,
        out_specs=tuple(specs),
        compiler_params=PARAMS,
        cost_estimate=LIGHT,
    )(*values)


def arrange_kernel(place, *refs):
    out = refs[-1]
    x, c = place[2], place[3]
    sign = 1 - 2 * c
    width = out.shape[1] // 8
    for step in range(NX):
        for block, turn, core in ((refs[step], sign, c), (refs[NX + step], -sign, 1 - c)):
            owner = lax.rem(x - turn * step + 2 * NX, NX) * 2 + core
            out[:, pl.ds(pl.multiple_of(owner * width, width), width)] = block[...]


def arrange(place, blocks):
    tokens, width = blocks[0].shape
    return pl.pallas_call(
        arrange_kernel,
        grid=(1,),
        out_shape=jax.ShapeDtypeStruct((tokens, width * 8), jnp.bfloat16),
        in_specs=[smem()] + [full(*block.shape) for block in blocks],
        out_specs=full(tokens, width * 8),
        compiler_params=PARAMS,
        cost_estimate=LIGHT,
    )(place, *blocks)


A_TILES = ROWS_A // TILE


A_TILES = ROWS_A // TILE


def lanes_of(place, z, dy):
    owner = z * NY + lax.rem(place[1] - dy + NY, NY)
    return pl.ds(pl.multiple_of(owner * 128, 128), 128)


def own_kernel(place, left, routed, factor, own, out, sides, later, picked):
    @pl.when(pl.program_id(0) == 0)
    def _():
        for z in range(NZ):
            lanes = pl.ds(z * 128, 128)
            picked[:, lanes] = left[:, lanes_of(place, z, 0)]
            sides[:, lanes] = left[:, lanes_of(place, z, 1)]
            sides[:, pl.ds((NZ + z) * 128, 128)] = left[:, lanes_of(place, z, -1)]
            later[:, lanes] = left[:, lanes_of(place, z, 2)]

    right = jnp.concatenate([own[z] for z in range(NZ)], axis=1)
    total = lax.dot_general(picked[...], right, LAST, preferred_element_type=jnp.float32)
    total += lax.dot_general(routed[...], factor[...], LAST, preferred_element_type=jnp.float32)
    out[...] = total


def sides_kernel(picked, partial, plus, minus, out):
    right = jnp.concatenate([side[z] for side in (plus, minus) for z in range(NZ)], axis=1)
    total = lax.dot_general(picked[...], right, LAST, preferred_element_type=jnp.float32)
    out[...] = total + partial[...]


def last_rows_kernel(place, left, routed, factor, blocks, out, right):
    for z in range(NZ):
        for dy in range(NY):
            right[:, lanes_of(place, z, dy)] = blocks[z, dy]
    total = lax.dot_general(left[...], right[...], LAST, preferred_element_type=jnp.float32)
    total += lax.dot_general(routed[...], factor[...], LAST, preferred_element_type=jnp.float32)
    out[...] = total.astype(out.dtype)


def late_kernel(picked, partial, low, high, base, out):
    del base
    blocks = [low[z] for z in range(NZ // 2)] + [high[z] for z in range(NZ // 2)]
    right = jnp.concatenate(blocks, axis=1)
    total = lax.dot_general(picked[...], right, LAST, preferred_element_type=jnp.float32)
    out[...] = (total + partial[...]).astype(out.dtype)


def whole(shape):
    return pl.BlockSpec(shape, lambda n: (0,) * len(shape), pipeline_mode=pl.Buffered(1))


def project_own(place, left, routed, factor, own):
    tokens, depth = left.shape
    used = depth // NY
    return pl.pallas_call(
        own_kernel,
        grid=(A_TILES,),
        out_shape=(
            jax.ShapeDtypeStruct((tokens, ROWS_A), jnp.float32),
            jax.ShapeDtypeStruct((tokens, 2 * used), jnp.bfloat16),
            jax.ShapeDtypeStruct((tokens, used), jnp.bfloat16),
        ),
        in_specs=[smem(), whole((tokens, depth)), whole((tokens, 128))]
        + [pl.BlockSpec((TILE, 128), lambda n: (n, 0))]
        + [pl.BlockSpec((NZ, TILE, 128), lambda n: (0, n, 0))],
        out_specs=(
            pl.BlockSpec((tokens, TILE), lambda n: (0, n)),
            pl.BlockSpec((tokens, 2 * used), lambda n: (0, 0)),
            pl.BlockSpec((tokens, used), lambda n: (0, 0)),
        ),
        scratch_shapes=[pltpu.VMEM((tokens, used), jnp.bfloat16)],
        compiler_params=PARAMS,
        cost_estimate=LIGHT,
    )(place, left, routed, factor, own)


def project_sides(picked, partial, plus, minus):
    tokens, depth = picked.shape
    return pl.pallas_call(
        sides_kernel,
        grid=(A_TILES,),
        out_shape=jax.ShapeDtypeStruct(partial.shape, jnp.float32),
        in_specs=[whole((tokens, depth)), pl.BlockSpec((tokens, TILE), lambda n: (0, n))]
        + [pl.BlockSpec((NZ, TILE, 128), lambda n: (0, n, 0))] * 2,
        out_specs=pl.BlockSpec((tokens, TILE), lambda n: (0, n)),
        compiler_params=PARAMS,
        cost_estimate=LIGHT,
    )(picked, partial, plus, minus)


def project_last_rows(place, left, routed, factor, blocks):
    tokens, depth = left.shape
    units = factor.shape[0]
    return pl.pallas_call(
        last_rows_kernel,
        grid=(units // TILE - A_TILES,),
        out_shape=jax.ShapeDtypeStruct((tokens, units), jnp.bfloat16),
        in_specs=[smem(), whole((tokens, depth)), whole((tokens, 128))]
        + [
            pl.BlockSpec((TILE, 128), lambda n: (n + A_TILES, 0)),
            pl.BlockSpec((NZ, NY, TILE, 128), lambda n: (0, 0, n, 0)),
        ],
        out_specs=pl.BlockSpec((tokens, TILE), lambda n: (0, n + A_TILES)),
        scratch_shapes=[pltpu.VMEM((TILE, depth), jnp.bfloat16)],
        compiler_params=PARAMS,
        cost_estimate=LIGHT,
    )(place, left, routed, factor, blocks)


def project_late(picked, partial, low, high, base):
    tokens, depth = picked.shape
    return pl.pallas_call(
        late_kernel,
        grid=(A_TILES,),
        out_shape=jax.ShapeDtypeStruct(base.shape, jnp.bfloat16),
        in_specs=[whole((tokens, depth)), pl.BlockSpec((tokens, TILE), lambda n: (0, n))]
        + [pl.BlockSpec((NZ // 2, TILE, 128), lambda n: (0, n, 0))] * 2
        + [pl.BlockSpec(memory_space=pl.ANY)],
        out_specs=pl.BlockSpec((tokens, TILE), lambda n: (0, n)),
        input_output_aliases={4: 0},
        compiler_params=PARAMS,
        cost_estimate=LIGHT,
    )(picked, partial, low, high, base)


def per_device(
    hidden,
    layer_output_gradient,
    frozen_down_weight,
    adapter_down_weight,
    adapter_up_weight,
    chosen_expert_index,
    gates,
):
    together = lambda *values: lax.optimization_barrier(values)
    dp_index = lax.axis_index("dp").astype(jnp.int32)
    tensor_index = lax.axis_index("tensor").astype(jnp.int32)
    place = jnp.stack(
        [lax.div(dp_index, NY), lax.rem(dp_index, NY), lax.div(tensor_index, 2), lax.rem(tensor_index, 2)]
    )
    tokens_here = hidden.shape[0]
    token_scale = float(tokens_here * NZ * NY) ** (-0.5)
    n = NZ * NY

    own, last = frozen_down_weight[:ROWS_A], frozen_down_weight[ROWS_A:]
    row = lax.all_gather(own, "dp", axis=0, axis_index_groups=Z_GROUPS)
    kept, sent = project_low_rank(
        place, hidden, adapter_down_weight, layer_output_gradient, adapter_up_weight
    )
    last, kept, sent = together(last, kept, sent)
    b1, b2, b3 = move_y(last, 1), move_y(last, 2), move_y(last, -1)
    near = [layer_output_gradient, turn_x(layer_output_gradient)]
    kept = kept + swap_core(sent)
    kept = kept + swap_x(kept, lambda x: x ^ 1)
    chosen, weights = copied(chosen_expert_index, gates)
    kept, chosen, weights = together(kept, chosen, weights)
    kept = kept + swap_x(kept, lambda x: 3 - x)
    b1, b2, b3, kept, near[1] = together(b1, b2, b3, kept, near[1])
    column = jnp.stack([last, b1, b2, b3])
    b_blocks = lax.all_gather(column, "dp", axis=0, axis_index_groups=Z_GROUPS)

    other = swap_core(kept)
    *chunks, routed, gate_gradient = route(
        place, kept, other, chosen, weights, hidden, layer_output_gradient
    )
    near.append(turn_x(near[-1]))

    came = [move_y(chunks[j], j) for j in range(1, NY)]
    parts = sum(chunk.astype(jnp.float32) for chunk in [chunks[0]] + came)
    row, parts, near[2] = together(row, parts, near[2])
    plus, minus = move_y(row, 1), move_y(row, -1)
    parts = lax.all_to_all(parts, "dp", 0, 0, tiled=True, axis_index_groups=Z_GROUPS)
    total = jnp.sum(parts, axis=0) * token_scale
    down_rows = hidden.shape[1] // n
    down = jnp.broadcast_to(total[:down_rows].astype(jnp.bfloat16)[None], (NZ, down_rows, 128))
    down = lax.all_to_all(down, "dp", 0, 0, tiled=True, axis_index_groups=Z_GROUPS)
    near.append(turn_x(near[-1]))
    left = arrange(place, near + [swap_core(block) for block in near])
    partial, side_left, late_left = project_own(place, left, routed, adapter_down_weight, row)
    plus, minus, partial, side_left, late_left, down, total = together(
        plus, minus, partial, side_left, late_left, down, total
    )

    half = NZ // 2
    low, high = move_y(plus[:half], 1), move_y(minus[half:], -1)
    partial = project_sides(side_left, partial, plus, minus)
    hidden_input_gradient = project_last_rows(place, left, routed, adapter_down_weight, b_blocks)
    hidden_input_gradient, low, high, partial, down, total = together(
        hidden_input_gradient, low, high, partial, down, total
    )
    came = [down] + [move_y(down, j) for j in range(1, NY)]
    pairs = [(d * 8 + t, (4 * t + d // 8) * 8 + d % 8) for d in range(n) for t in range(8)]
    up_factor_gradient = lax.ppermute(total[down_rows:], ("dp", "tensor"), pairs).T
    hidden_input_gradient = project_late(late_left, partial, low, high, hidden_input_gradient)
    came = jnp.stack([came[(3 - i) % NY] for i in range(2 * NY - 1)])
    came = lax.dynamic_slice_in_dim(came, 3 - place[1], NY, axis=0)
    down_factor_gradient = came.transpose(1, 0, 2, 3).reshape(-1, 128).astype(jnp.float32)
    return (hidden_input_gradient, down_factor_gradient, up_factor_gradient, gate_gradient)


def solution(mesh):
    return jax.shard_map(
        per_device,
        mesh=mesh,
        in_specs=(
            P("dp", "tensor"),
            P("dp", "tensor"),
            P("tensor", "dp"),
            P("tensor", None),
            P(),
            P("dp", None),
            P("dp", None),
        ),
        out_specs=(P("dp", "tensor"), P("tensor", None), P(None, ("dp", "tensor")), P("dp", None)),
        check_vma=False,
    )
```
